256 devices in a mesh: lat: 16 (over y_hi, z), lon: 4 (over y_lo, core), dp: 4 (over x).
Axes of the slice: x: 4, y: 4 (y_hi: 2, y_lo: 2; y = y_hi * 2 + y_lo), z: 8, core: 2. Of those that a mesh axis runs over, the one named last changes fastest.
Arguments:
- inputs: bfloat16 [4, 4, 192, 24, 1024], P('dp', None, 'lat', 'lon'), may hold values from -8 to 8
- cotangent: bfloat16 [4, 4, 192, 24, 1024], P('dp', None, 'lat', 'lon'), may hold values from -6 to 6
- gain: float32 [1024], replicated, may hold values from 0.1 to 1.9
- w_qkv: bfloat16 [1024, 1536], replicated, may hold values from -0.125 to 0.125
- w_proj: bfloat16 [512, 1024], replicated, may hold values from -0.25 to 0.25
- window_ids: int32 [4, 192, 24], P(None, 'lat', 'lon'), may hold values from 0 to 3, as said below
Outputs:
- outputs: bfloat16 [4, 4, 192, 24, 1024], P('dp', None, 'lat', 'lon')
- input_grad: bfloat16 [4, 4, 192, 24, 1024], P('dp', None, 'lat', 'lon')
- qkv_grad: float32 [1024, 1536], P(('lat', 'lon', 'dp'))
- proj_grad: float32 [512, 1024], P(None, ('lat', 'lon', 'dp'))
- gain_grad: float32 [1024], P(('lat', 'lon', 'dp'))
The draws below stay inside these ranges and needn't reach their ends.
Inputs may be any that keep to these rules, and one draw needn't show every extreme that they name: `window_ids`: inside each window of the shifted grid the labels are equal over levels and form four rectangles cut by one latitude row and one longitude column, labelled 0 to 3.
All inputs are finite; a program needn't handle non-finite values.
Results may differ from the reference program's by a relative error of at most 0.014.
The reference program's roundings to bfloat16 on the way count: a program that leaves them out, or rounds other values in their place, can miss the bound.
Values may be sent and summed in bfloat16 or wider, within the bound.
A program may use at most 128 MiB of HBM per device.

```python
import math
import jax
import jax.numpy as jnp
from jax import lax

D = 1024
HEADS = 8
HSZ = 64
LEV = 4
WL = 2
WA = 12
WO = 6
BATCH = 4
NLAT = 192
NLON = 24


def draw_inputs(key, part):
    key = jax.random.fold_in(key, 11)
    key_noise = jax.random.fold_in(key, 0)
    values = jnp.clip(jax.random.normal(key_noise, (BATCH, LEV, NLAT, NLON, D), jnp.float32), -6.0, 6.0)
    return values.astype(jnp.bfloat16)


def draw_w_qkv(key, part):
    key = jax.random.fold_in(key, 13)
    key_base = jax.random.fold_in(key, 0)
    scale_in = D ** (-0.5)
    matrix = jnp.clip(jax.random.normal(key_base, (D, 3 * HEADS * HSZ), jnp.float32) * scale_in, -0.125, 0.125)
    return matrix.astype(jnp.bfloat16)


def draw_window_ids(key, part):
    key = jax.random.fold_in(key, 7)
    key_rows, key_cols = jax.random.split(key)
    lev_windows = LEV // WL
    lat_windows = NLAT // WA
    lon_windows = NLON // WO
    cut_rows = jax.random.randint(key_rows, (lev_windows, lat_windows, lon_windows), 1, WA)
    cut_cols = jax.random.randint(key_cols, (lev_windows, lat_windows, lon_windows), 1, WO)
    row_index = jnp.arange(WA, dtype=jnp.int32)
    col_index = jnp.arange(WO, dtype=jnp.int32)
    upper_part = (row_index[None, None, None, :, None] >= cut_rows[:, :, :, None, None]).astype(jnp.int32)
    right_part = (col_index[None, None, None, None, :] >= cut_cols[:, :, :, None, None]).astype(jnp.int32)
    labels = upper_part * 2 + right_part
    labels = jnp.broadcast_to(labels[:, None], (lev_windows, WL, lat_windows, lon_windows, WA, WO))
    labels = labels.transpose(0, 1, 2, 4, 3, 5)
    return labels.reshape(LEV, NLAT, NLON).astype(jnp.int32)


def level_of(rng, shape, cuts, smallest, top_value):
    factor_of, own = 1.0, jax.random.fold_in(rng, 6)
    for dim, blocks in cuts:
        heights = jnp.exp(jax.random.uniform(jax.random.fold_in(own, dim), (blocks,), jnp.float32, smallest / len(cuts), top_value / len(cuts)))
        factor_of = factor_of * jnp.repeat(heights, shape[dim] // blocks).reshape([-1 if axis == dim else 1 for axis in range(len(shape))])
    return factor_of


def noise(key, shape, scale, most, cuts=(), held_as=jnp.bfloat16):
    drawn = jax.random.normal(key, shape, jnp.float32) * scale
    if len(cuts) > 0:
        drawn = level_of(key, shape, cuts, -0.22, 0.18) * drawn
    return jnp.clip(drawn, min=-most, max=most).astype(held_as)


def setup_inputs(seed: int = 0) -> dict:
    streams_of = jax.random.split(jax.random.key(seed), 7)
    inputs = draw_inputs(jax.random.fold_in(streams_of[6], 71), 0)
    cotangent = noise(streams_of[1], (BATCH, LEV, NLAT, NLON, D), 1.0, 6.0, ((0, 4), (2, 16), (3, 4)))
    gain = jnp.clip(1.0 + 0.18 * jax.random.normal(streams_of[2], (D,), jnp.float32), 0.1, 1.9)
    w_qkv = draw_w_qkv(jax.random.fold_in(streams_of[6], 71), 0)
    w_proj = noise(streams_of[4], (HEADS * HSZ, D), (HEADS * HSZ) ** -0.5, 0.25)
    window_ids = draw_window_ids(jax.random.fold_in(streams_of[6], 71), 0)
    return {"inputs": inputs, "cotangent": cotangent, "gain": gain, "w_qkv": w_qkv, "w_proj": w_proj, "window_ids": window_ids}


def to_windows(array):
    dims = array.shape
    array = array.reshape(dims[0], dims[1] // WL, WL, dims[2] // WA, WA, dims[3] // WO, WO, dims[4])
    array = array.transpose(0, 1, 3, 5, 2, 4, 6, 7)
    return array.reshape(-1, WL * WA * WO, dims[4])

def from_windows(windowed, grid_shape):
    array = windowed.reshape(grid_shape[0], grid_shape[1] // WL, grid_shape[2] // WA, grid_shape[3] // WO, WL, WA, WO, grid_shape[4])
    return array.transpose(0, 1, 4, 2, 5, 3, 6, 7).reshape(grid_shape)

def window_core(queries, key_rows, values, same_group, d_out):
    score_scale = queries.shape[-1] ** (-0.5)
    scores = jnp.einsum('gqhe,gkhe->ghqk', queries.astype(jnp.float32), key_rows.astype(jnp.float32)) * score_scale
    scores = jnp.where(same_group[:, None], scores, -1e+30)
    scores = scores - lax.optimization_barrier(jnp.max(scores, axis=-1, keepdims=True))
    exp_scores = jnp.exp(scores)
    attn_prob = exp_scores / lax.optimization_barrier(jnp.sum(exp_scores, axis=-1, keepdims=True))
    prob_half = attn_prob.astype(jnp.bfloat16)
    attended = jnp.einsum('ghqk,gkhe->gqhe', prob_half.astype(jnp.float32), values.astype(jnp.float32)).astype(jnp.bfloat16)
    d_prob = jnp.einsum('gqhe,gkhe->ghqk', d_out.astype(jnp.float32), values.astype(jnp.float32))
    d_values = jnp.einsum('ghqk,gqhe->gkhe', prob_half.astype(jnp.float32), d_out.astype(jnp.float32)).astype(jnp.bfloat16)
    d_scores = (attn_prob * (d_prob - lax.optimization_barrier(jnp.sum(attn_prob * d_prob, axis=-1, keepdims=True))) * score_scale).astype(jnp.bfloat16)
    d_queries = jnp.einsum('ghqk,gkhe->gqhe', d_scores.astype(jnp.float32), key_rows.astype(jnp.float32)).astype(jnp.bfloat16)
    d_keys = jnp.einsum('ghqk,gqhe->gkhe', d_scores.astype(jnp.float32), queries.astype(jnp.float32)).astype(jnp.bfloat16)
    return (attended, d_queries, d_keys, d_values)

def block_terms(x_win, dy_win, gain, w_qkv, w_proj, same_group):
    windows_n, span, width = x_win.shape
    x_flat = x_win.reshape(-1, width).astype(jnp.float32)
    token_mean = lax.optimization_barrier(jnp.mean(x_flat, axis=-1, keepdims=True))
    centred = x_flat - token_mean
    inv_std = lax.rsqrt(lax.optimization_barrier(jnp.mean(centred * centred, axis=-1, keepdims=True)) + 1e-05)
    normed = centred * inv_std
    hidden = (normed * gain).astype(jnp.bfloat16)
    projected = jnp.dot(hidden, w_qkv, preferred_element_type=jnp.float32).astype(jnp.bfloat16)
    projected = projected.reshape(windows_n, span, 3, HEADS, HSZ)
    dy_flat = dy_win.reshape(-1, width)
    d_attended = jnp.dot(dy_flat, w_proj.T, preferred_element_type=jnp.float32).astype(jnp.bfloat16)
    d_attended = d_attended.reshape(windows_n, span, HEADS, HSZ)
    group_size = LEV // WL * (NLON // WO)
    operands = (projected[:, :, 0], projected[:, :, 1], projected[:, :, 2], same_group, d_attended)
    grouped = tuple((item.reshape((-1, group_size) + item.shape[1:]) for item in operands))

    def one_group(pieces):
        return window_core(pieces[0], pieces[1], pieces[2], pieces[3], pieces[4])
    results = lax.map(one_group, grouped)
    attended, d_q, d_k, d_v = tuple((item.reshape((-1,) + item.shape[2:]) for item in results))
    att_flat = attended.reshape(-1, HEADS * HSZ)
    y_flat = (x_flat + jnp.dot(att_flat, w_proj, preferred_element_type=jnp.float32)).astype(jnp.bfloat16)
    proj_term = jnp.dot(att_flat.T, dy_flat, preferred_element_type=jnp.float32)
    d_qkv = jnp.stack((d_q, d_k, d_v), axis=2).reshape(-1, 3 * HEADS * HSZ)
    qkv_term = jnp.dot(hidden.T, d_qkv, preferred_element_type=jnp.float32)
    d_hidden = jnp.dot(d_qkv, w_qkv.T, preferred_element_type=jnp.float32)
    gain_term = lax.optimization_barrier(jnp.sum(d_hidden * normed, axis=0))
    d_normed = d_hidden * gain
    correction = d_normed - lax.optimization_barrier(jnp.mean(d_normed, axis=-1, keepdims=True)) - normed * lax.optimization_barrier(jnp.mean(d_normed * normed, axis=-1, keepdims=True))
    dx_flat = (dy_flat.astype(jnp.float32) + inv_std * correction).astype(jnp.bfloat16)
    return (y_flat, dx_flat, qkv_term, proj_term, gain_term)

def reference(inputs, cotangent, gain, w_qkv, w_proj, window_ids):
    half_a = WA // 2
    half_o = WO // 2
    grid_shape = inputs.shape
    xs = jnp.roll(inputs, (-half_a, -half_o), axis=(2, 3))
    dys = jnp.roll(cotangent, (-half_a, -half_o), axis=(2, 3))
    x_win = to_windows(xs)
    dy_win = to_windows(dys)
    per_sample = x_win.shape[0] // grid_shape[0]
    x_win = x_win.reshape((grid_shape[0], per_sample) + x_win.shape[1:])
    dy_win = dy_win.reshape((grid_shape[0], per_sample) + dy_win.shape[1:])
    ids_win = to_windows(window_ids[None, :, :, :, None])[:, :, 0]
    same_group = ids_win[:, :, None] == ids_win[:, None, :]

    def one_sample(pieces):
        return block_terms(pieces[0], pieces[1], gain, w_qkv, w_proj, same_group)
    y_all, dx_all, qkv_terms, proj_terms, gain_terms = lax.map(one_sample, (x_win, dy_win))
    ys = from_windows(y_all, grid_shape)
    dxs = from_windows(dx_all, grid_shape)
    outputs = jnp.roll(ys, (half_a, half_o), axis=(2, 3))
    input_grad = jnp.roll(dxs, (half_a, half_o), axis=(2, 3))
    cells = grid_shape[0] * grid_shape[1] * grid_shape[2] * grid_shape[3]
    scale_back = 1.0 / math.sqrt(cells)
    qkv_grad = lax.optimization_barrier(jnp.sum(qkv_terms, axis=0)) * scale_back
    proj_grad = lax.optimization_barrier(jnp.sum(proj_terms, axis=0)) * scale_back
    gain_grad = lax.optimization_barrier(jnp.sum(gain_terms, axis=0)) * scale_back
    return (outputs, input_grad, qkv_grad, proj_grad, gain_grad)
```

```python
import functools
import math

import jax
import jax.numpy as jnp
from jax import lax
from jax.experimental import pallas as pl
from jax.experimental.pallas import tpu as pltpu
from jax.sharding import PartitionSpec as P

HEADS = 8
HSZ = 64
WA = 12
WO = 6
HALF_A = WA // 2
HALF_O = WO // 2
LEV = 4
CELLS = WA * WO
ROWS = CELLS * LEV
SPAN = 2 * CELLS
D = 1024
QKV = 3 * HEADS * HSZ
ATT = HEADS * HSZ
COLS = QKV + ATT
MESH = pl.DeviceIdType.MESH
F32 = jnp.float32
BF16 = jnp.bfloat16


def place():
    return lax.axis_index("lat"), lax.axis_index("lon"), lax.axis_index("dp")


def wrap(value, size):
    return lax.rem(value + size, size)


def partners():
    lat, lon, dp = place()
    odd = lax.rem(lon, 2)
    turn = 2 * odd - 1
    to = [
        (wrap(lat + turn, 16), lon, dp),
        (lat, wrap(lon - 1, 4), dp),
        (wrap(lat - turn, 16), wrap(lon - 1, 4), dp),
    ]
    source = [
        (wrap(lat - turn, 16), lon, dp),
        (lat, wrap(lon + 1, 4), dp),
        (wrap(lat - turn, 16), wrap(lon + 1, 4), dp),
    ]
    sent = [(odd, 1), (odd, 0), (1 - odd, 0)]
    taken = [(odd, 1), (1 - odd, 0), (odd, 0)]
    own = (1 - odd, 1)
    return odd, to, source, sent, taken, own


def block_part(ref, part):
    return ref.at[pl.ds(part[0] * HALF_A, HALF_A), pl.ds(part[1] * HALF_O, HALF_O)]


def window_part(ref, part):
    return ref.at[pl.ds((1 - part[0]) * HALF_A, HALF_A), pl.ds((1 - part[1]) * HALF_O, HALF_O)]


def greet(devices, count):
    barrier = pltpu.get_barrier_semaphore()
    for device in devices:
        pl.semaphore_signal(barrier, inc=1, device_id=device, device_id_type=MESH)
    pl.semaphore_wait(barrier, count)


def remote(src, dst, send_sem, recv_sem, device):
    return pltpu.make_async_remote_copy(
        src_ref=src, dst_ref=dst, send_sem=send_sem, recv_sem=recv_sem, device_id=device, device_id_type=MESH
    )


def halo_kernel(x_ref, dy_ref, ids_ref, xw_ref, dyw_ref, idw_ref, send_sem, recv_sem, own_sem):
    odd, to, source, sent, taken, own = partners()
    greet(source, 3)
    copies = []
    for n, (src, dst) in enumerate(((x_ref, xw_ref), (dy_ref, dyw_ref))):
        for k in range(3):
            copies.append(
                remote(
                    block_part(src, sent[k]),
                    window_part(dst, sent[k]),
                    send_sem.at[3 * n + k],
                    recv_sem.at[3 * n + k],
                    to[k],
                )
            )
            copies[-1].start()
    local = [
        pltpu.make_async_copy(block_part(x_ref, own), window_part(xw_ref, own), own_sem.at[0]),
        pltpu.make_async_copy(block_part(dy_ref, own), window_part(dyw_ref, own), own_sem.at[1]),
    ]
    for copy in local:
        copy.start()

    @pl.when(odd == 1)
    def _():
        labels = remote(ids_ref, idw_ref, send_sem.at[6], recv_sem.at[6], to[0])
        labels.start()
        labels.wait()

    @pl.when(odd == 0)
    def _():
        labels = pltpu.make_async_copy(ids_ref, idw_ref, own_sem.at[2])
        labels.start()
        labels.wait()

    for copy in copies + local:
        copy.wait()


def halo(x, dy, ids):
    block = jax.ShapeDtypeStruct((WA, WO, LEV, D), BF16)
    return pl.pallas_call(
        halo_kernel,
        out_shape=(block, block, jax.ShapeDtypeStruct(ids.shape, ids.dtype)),
        in_specs=[pl.BlockSpec(memory_space=pl.ANY)] * 3,
        out_specs=(pl.BlockSpec(memory_space=pl.ANY),) * 3,
        scratch_shapes=[
            pltpu.SemaphoreType.DMA((7,)),
            pltpu.SemaphoreType.DMA((7,)),
            pltpu.SemaphoreType.DMA((3,)),
        ],
        compiler_params=pltpu.CompilerParams(collective_id=1, has_side_effects=True),
        name="halo_in",
    )(x, dy, ids)


def dot(a, b):
    return jnp.dot(a, b, preferred_element_type=F32)


def dot_nt(a, b):
    return lax.dot_general(a, b, (((1,), (1,)), ((), ())), preferred_element_type=F32)


def dot_tn(a, b):
    return lax.dot_general(a, b, (((0,), (0,)), ((), ())), preferred_element_type=F32)


def spread(block_ref, wide):
    def step(c, _):
        pair = jnp.concatenate((block_ref[2 * c].astype(F32), block_ref[2 * c + 1].astype(F32)), axis=0)
        for j in range(D // 128):
            wide[j, pl.ds(pl.multiple_of(8 * c, 8), 8), :] = pair[:, 128 * j : 128 * j + 128]
        return 0

    lax.fori_loop(0, CELLS // 2, step, 0, unroll=4)


def gather(wide, block_ref):
    def step(c, _):
        pair = jnp.concatenate([wide[j, pl.ds(pl.multiple_of(8 * c, 8), 8), :] for j in range(D // 128)], axis=1)
        block_ref[2 * c] = pair[:LEV].astype(BF16)
        block_ref[2 * c + 1] = pair[LEV:].astype(BF16)
        return 0

    lax.fori_loop(0, CELLS // 2, step, 0, unroll=4)


def load_level(wide, level):
    return jnp.concatenate([wide[j, pl.ds(level, CELLS, stride=LEV), :] for j in range(D // 128)], axis=1)


def store_level(wide, level, value):
    for j in range(D // 128):
        wide[j, pl.ds(level, CELLS, stride=LEV), :] = value[:, 128 * j : 128 * j + 128]


def rows_of(level):
    return pl.ds(level * CELLS, CELLS)


def core_kernel(
    xw_ref,
    dyw_ref,
    lab_ref,
    gain_ref,
    wqkv_ref,
    wproj_ref,
    y_ref,
    dx_ref,
    g_ref,
    wide,
    xs,
    normed,
    inv,
    hid,
    dys,
    qkv,
    datt,
    att,
    dqkv,
    same,
):
    gain = gain_ref[...]
    spread(xw_ref, wide)
    for level in range(LEV):
        x = load_level(wide, level)
        centred = x - jnp.mean(x, axis=-1, keepdims=True)
        inv_std = lax.rsqrt(jnp.mean(centred * centred, axis=-1, keepdims=True) + 1e-05)
        unit = centred * inv_std
        xs[rows_of(level), :] = x
        normed[rows_of(level), :] = unit
        inv[rows_of(level), :] = jnp.broadcast_to(inv_std, (CELLS, 128))
        hid[rows_of(level), :] = (unit * gain).astype(BF16)
    spread(dyw_ref, wide)
    for level in range(LEV):
        dys[rows_of(level), :] = load_level(wide, level).astype(BF16)
    qkv[...] = dot(hid[...], wqkv_ref[...]).astype(BF16)
    datt[...] = dot_nt(dys[...], wproj_ref[...]).astype(BF16)
    for w in range(2):
        row = jnp.broadcast_to(lab_ref[w : w + 1, :], (128, 128))
        one = (row == row.T)[:CELLS, :CELLS].astype(F32)
        two = jnp.concatenate((one, one), axis=1)
        same[w] = jnp.concatenate((two, two), axis=0)

    low = lax.broadcasted_iota(jnp.int32, (1, 128), 1) < HSZ

    def heads(step, _):
        for w in range(2):
            rows = pl.ds(w * SPAN, SPAN)
            at = pl.multiple_of(step * 128, 128)
            q2 = qkv[rows, pl.ds(at, 128)]
            k2 = qkv[rows, pl.ds(ATT + at, 128)]
            v2 = qkv[rows, pl.ds(2 * ATT + at, 128)]
            o2 = datt[rows, pl.ds(at, 128)]
            apart = []
            for keep in (low, jnp.logical_not(low)):
                keep_w = jnp.broadcast_to(keep, (SPAN, 128))
                qh = jnp.where(keep_w, q2.astype(F32) * (HSZ**-0.5), 0.0).astype(BF16)
                oh = jnp.where(keep_w, o2.astype(F32), 0.0).astype(BF16)
                scores = jnp.where(same[w] > 0.5, dot_nt(k2, qh), -1e30)
                scores = scores - jnp.max(scores, axis=0, keepdims=True)
                weight = jnp.exp(scores)
                prob = weight * (1.0 / jnp.sum(weight, axis=0, keepdims=True))
                prob_b = prob.astype(BF16)
                d_prob = dot_nt(v2, oh)
                inner = jnp.sum(prob * d_prob, axis=0, keepdims=True)
                d_score = (prob * (d_prob - inner) * (HSZ**-0.5)).astype(BF16)
                apart.append((dot_tn(prob_b, v2), dot_tn(d_score, k2), dot(d_score, q2), dot(prob_b, o2)))
            both = [jnp.where(low, first, second).astype(BF16) for first, second in zip(*apart)]
            att[rows, pl.ds(at, 128)] = both[0]
            dqkv[rows, pl.ds(at, 128)] = both[1]
            dqkv[rows, pl.ds(ATT + at, 128)] = both[2]
            dqkv[rows, pl.ds(2 * ATT + at, 128)] = both[3]
        return 0

    lax.fori_loop(0, HEADS // 2, heads, 0)

    for level in range(LEV):
        store_level(wide, level, xs[rows_of(level), :] + dot(att[rows_of(level), :], wproj_ref[...]))
    gather(wide, y_ref)
    for level in range(LEV):
        g = dot_nt(dqkv[rows_of(level), :], wqkv_ref[...]) * gain
        unit = normed[rows_of(level), :]
        correction = g - jnp.mean(g, axis=-1, keepdims=True) - unit * jnp.mean(g * unit, axis=-1, keepdims=True)
        inv_std = inv[rows_of(level), 0:1]
        store_level(wide, level, dys[rows_of(level), :].astype(F32) + inv_std * correction)
    gather(wide, dx_ref)
    for block in range(D // 128):
        at = block * 128
        left = dot_tn(hid[:, at : at + 128], dqkv[...]).astype(BF16)
        right = dot_tn(dys[:, at : at + 128], att[...]).astype(BF16)
        g_ref[pl.ds(8 * block, 8), :, 0:QKV] = left.reshape(8, 16, QKV)
        g_ref[pl.ds(8 * block, 8), :, QKV:COLS] = right.reshape(8, 16, ATT)


def core(xw, dyw, labels, gain, w_qkv, w_proj):
    block = jax.ShapeDtypeStruct((CELLS, LEV, D), BF16)
    vmem = pl.BlockSpec(memory_space=pltpu.VMEM)
    return pl.pallas_call(
        core_kernel,
        out_shape=(block, block, jax.ShapeDtypeStruct((64, 16, COLS), BF16)),
        in_specs=[vmem] * 6,
        out_specs=(vmem,) * 3,
        scratch_shapes=[
            pltpu.VMEM((D // 128, ROWS, 128), F32),
            pltpu.VMEM((ROWS, D), F32),
            pltpu.VMEM((ROWS, D), F32),
            pltpu.VMEM((ROWS, 128), F32),
            pltpu.VMEM((ROWS, D), BF16),
            pltpu.VMEM((ROWS, D), BF16),
            pltpu.VMEM((ROWS, QKV), BF16),
            pltpu.VMEM((ROWS, ATT), BF16),
            pltpu.VMEM((ROWS, ATT), BF16),
            pltpu.VMEM((ROWS, QKV), BF16),
            pltpu.VMEM((2, SPAN, SPAN), F32),
        ],
        compiler_params=pltpu.CompilerParams(vmem_limit_bytes=48 * 2**20),
        name="window_core",
    )(xw, dyw, labels, gain, w_qkv, w_proj)


def send_all(list_of):
    for copy in list_of:
        copy.start()
    return list_of


def wait_all(list_of):
    for copy in list_of:
        copy.wait()


def tail_kernel(
    yw_ref,
    dxw_ref,
    g_ref,
    y_ref,
    dx_ref,
    out_ref,
    mine,
    r1,
    sa,
    sb,
    ra,
    rb,
    ta,
    tb,
    r3a,
    r3b,
    u,
    r4,
    halo_send,
    halo_recv,
    own_sem,
    pair_sem,
    send2,
    recv2,
    send3,
    recv3,
    send4,
    recv4,
):
    lat, lon, dp = place()
    y_hi, z = lat // 8, lax.rem(lat, 8)
    y_lo, chip_core = lon // 2, lax.rem(lon, 2)
    y_pos = 2 * y_hi + y_lo
    pair = (lat, y_lo * 2 + 1 - chip_core, dp)
    along_x = [(lat, lon, lax.rem(dp + k, 4)) for k in range(1, 4)]
    along_y = []
    for k in range(1, 4):
        other = lax.rem(y_pos + k, 4)
        along_y.append((other // 2, lax.rem(other, 2)))
    y_devices = [(hi * 8 + z, lo * 2 + chip_core, dp) for hi, lo in along_y]
    along_z = [lax.rem(z + k, 8) for k in range(1, 8)]
    z_devices = [(y_hi * 8 + other, lon, dp) for other in along_z]
    odd, to, source, sent, taken, own = partners()

    greet(to + [pair] + along_x + y_devices + z_devices, 3 + 1 + 3 + 3 + 7)

    first = remote(g_ref.at[:, :, 1 - chip_core], r1, pair_sem.at[0], pair_sem.at[1], pair)
    first.start()
    own_half = pltpu.make_async_copy(g_ref.at[:, :, chip_core], mine, pair_sem.at[2])
    own_half.start()
    back = []
    for n, (src, dst) in enumerate(((yw_ref, y_ref), (dxw_ref, dx_ref))):
        for k in range(3):
            back.append(
                remote(
                    window_part(src, taken[k]),
                    block_part(dst, taken[k]),
                    halo_send.at[3 * n + k],
                    halo_recv.at[3 * n + k],
                    source[k],
                )
            )
            back[-1].start()
    local = [
        pltpu.make_async_copy(window_part(yw_ref, own), block_part(y_ref, own), own_sem.at[0]),
        pltpu.make_async_copy(window_part(dxw_ref, own), block_part(dx_ref, own), own_sem.at[1]),
    ]
    send_all(local)
    own_half.wait()
    first.wait()

    half = COLS // 2

    def add_pair(n, _):
        i, j = n // 2, lax.rem(n, 2)
        total = mine[i, j].astype(F32) + r1[i, j].astype(F32)
        for k in range(4):
            sa[k, i, j] = total[4 * k : 4 * k + 4, :half].astype(BF16)
        sb[i // 8, lax.rem(i, 8), j] = total[:, half:].astype(BF16)
        return 0

    lax.fori_loop(0, 32, add_pair, 0)

    stage2 = []
    for k in range(3):
        stage2.append(remote(sa.at[along_x[k][2]], ra.at[k], send2.at[k], recv2.at[k], along_x[k]))
        hi, lo = along_y[k]
        stage2.append(remote(sb.at[hi, :, lo], rb.at[k], send2.at[3 + k], recv2.at[3 + k], y_devices[k]))
    send_all(stage2)
    wait_all(stage2)

    def add_x(n, _):
        i, j = n // 2, lax.rem(n, 2)
        total = sa[dp, i, j].astype(F32)
        for k in range(3):
            total = total + ra[k, i, j].astype(F32)
        ta[i // 8, lax.rem(i, 8), j] = total.astype(BF16)
        return 0

    lax.fori_loop(0, 32, add_x, 0)

    def add_y(i, _):
        total = sb[y_hi, i, y_lo].astype(F32)
        for k in range(3):
            total = total + rb[k, i].astype(F32)
        for k in range(4):
            tb[k, i] = total[4 * k : 4 * k + 4].astype(BF16)
        return 0

    lax.fori_loop(0, 8, add_y, 0)

    stage3 = []
    for k in range(3):
        hi, lo = along_y[k]
        stage3.append(remote(ta.at[hi, :, lo], r3a.at[k], send3.at[k], recv3.at[k], y_devices[k]))
        stage3.append(remote(tb.at[along_x[k][2]], r3b.at[k], send3.at[3 + k], recv3.at[3 + k], along_x[k]))
    send_all(stage3)
    wait_all(stage3)

    def add_last(i, _):
        left = ta[y_hi, i, y_lo].astype(F32)
        right = tb[dp, i].astype(F32)
        for k in range(3):
            left = left + r3a[k, i].astype(F32)
            right = right + r3b[k, i].astype(F32)
        u[i, :, 0:half] = left.astype(BF16)
        u[i, :, half:COLS] = right.astype(BF16)
        return 0

    lax.fori_loop(0, 8, add_last, 0)

    stage4 = []
    for k in range(7):
        stage4.append(remote(u.at[along_z[k]], r4.at[k], send4.at[k], recv4.at[k], z_devices[k]))
    send_all(stage4)
    wait_all(stage4)
    total = u[z].astype(F32)
    for k in range(7):
        total = total + r4[k].astype(F32)
    out_ref[...] = total * (1.0 / math.sqrt(73728))
    wait_all(back)
    wait_all(local)


def tail(yw, dxw, g):
    block = jax.ShapeDtypeStruct((WA, WO, LEV, D), BF16)
    half = COLS // 2
    any_space = pl.BlockSpec(memory_space=pl.ANY)
    dma = pltpu.SemaphoreType.DMA
    return pl.pallas_call(
        tail_kernel,
        out_shape=(block, block, jax.ShapeDtypeStruct((4, COLS), F32)),
        in_specs=[any_space] * 3,
        out_specs=(any_space, any_space, pl.BlockSpec(memory_space=pltpu.VMEM)),
        scratch_shapes=[
            pltpu.VMEM((16, 2, 16, COLS), BF16),
            pltpu.VMEM((16, 2, 16, COLS), BF16),
            pltpu.VMEM((4, 16, 2, 4, half), BF16),
            pltpu.VMEM((2, 8, 2, 16, half), BF16),
            pltpu.VMEM((3, 16, 2, 4, half), BF16),
            pltpu.VMEM((3, 8, 16, half), BF16),
            pltpu.VMEM((2, 8, 2, 4, half), BF16),
            pltpu.VMEM((4, 8, 4, half), BF16),
            pltpu.VMEM((3, 8, 4, half), BF16),
            pltpu.VMEM((3, 8, 4, half), BF16),
            pltpu.VMEM((8, 4, COLS), BF16),
            pltpu.VMEM((7, 4, COLS), BF16),
            dma((6,)),
            dma((6,)),
            dma((2,)),
            dma((3,)),
            dma((6,)),
            dma((6,)),
            dma((6,)),
            dma((6,)),
            dma((7,)),
            dma((7,)),
        ],
        compiler_params=pltpu.CompilerParams(
            collective_id=2, has_side_effects=True, vmem_limit_bytes=32 * 2**20
        ),
        name="halo_out_and_sum",
    )(yw, dxw, g)


def cells_first(block):
    return block.transpose(0, 2, 3, 1, 4).reshape(WA, WO, LEV, D)


def on_device(inputs, cotangent, gain, w_qkv, w_proj, window_ids):
    x = cells_first(inputs)
    dy = cells_first(cotangent)
    ids = jnp.stack((window_ids[0].reshape(CELLS), window_ids[2].reshape(CELLS)))
    ids = jnp.pad(ids, ((0, 6), (0, 128 - CELLS)))
    xw, dyw, idw = halo(x, dy, ids)
    flat = (CELLS, LEV, D)
    yw, dxw, g = core(xw.reshape(flat), dyw.reshape(flat), idw, gain.reshape(1, D), w_qkv, w_proj)
    grid = (WA, WO, LEV, D)
    y, dx, share = tail(yw.reshape(grid), dxw.reshape(grid), g.reshape(16, 2, 2, 16, COLS))
    lat, lon, dp = place()
    first_row = 4 * (lat * 16 + lon * 4 + dp)
    qkv_part = share[:, :QKV]
    proj_part = share[:, QKV:].T
    w_rows = lax.dynamic_slice(w_qkv, (first_row, 0), (4, QKV)).astype(F32)
    gain_part = jnp.sum(w_rows * qkv_part, axis=-1) / lax.dynamic_slice(gain, (first_row,), (4,))
    back = lambda block: block[None].transpose(0, 3, 1, 2, 4)
    return back(y), back(dx), qkv_part, proj_part, gain_part


def solution(mesh):
    return jax.shard_map(
        on_device,
        mesh=mesh,
        in_specs=(
            P("dp", None, "lat", "lon", None),
            P("dp", None, "lat", "lon", None),
            P(),
            P(),
            P(),
            P(None, "lat", "lon"),
        ),
        out_specs=(
            P("dp", None, "lat", "lon", None),
            P("dp", None, "lat", "lon", None),
            P(("lat", "lon", "dp"), None),
            P(None, ("lat", "lon", "dp")),
            P(("lat", "lon", "dp")),
        ),
        check_vma=False,
    )
```

```python
import functools
import math

import jax
import jax.numpy as jnp
from jax import lax
from jax.experimental import pallas as pl
from jax.experimental.pallas import tpu as pltpu
from jax.sharding import PartitionSpec as P

HEADS = 8
HSZ = 64
WA = 12
WO = 6
HALF_A = WA // 2
HALF_O = WO // 2
LEV = 4
CELLS = WA * WO
ROWS = CELLS * LEV
SPAN = 2 * CELLS
D = 1024
QKV = 3 * HEADS * HSZ
ATT = HEADS * HSZ
COLS = QKV + ATT
CHUNKS = HEADS // 2
WIDE = COLS // CHUNKS
MESH = pl.DeviceIdType.MESH
F32 = jnp.float32
BF16 = jnp.bfloat16


def place():
    return lax.axis_index("lat"), lax.axis_index("lon"), lax.axis_index("dp")


def wrap(value, size):
    return lax.rem(value + size, size)


def partners():
    lat, lon, dp = place()
    odd = lax.rem(lon, 2)
    turn = 2 * odd - 1
    to = [
        (wrap(lat + turn, 16), lon, dp),
        (lat, wrap(lon - 1, 4), dp),
        (wrap(lat - turn, 16), wrap(lon - 1, 4), dp),
    ]
    source = [
        (wrap(lat - turn, 16), lon, dp),
        (lat, wrap(lon + 1, 4), dp),
        (wrap(lat - turn, 16), wrap(lon + 1, 4), dp),
    ]
    sent = [(odd, 1), (odd, 0), (1 - odd, 0)]
    taken = [(odd, 1), (1 - odd, 0), (odd, 0)]
    own = (1 - odd, 1)
    return odd, to, source, sent, taken, own


def block_part(ref, part):
    return ref.at[pl.ds(part[0] * HALF_A, HALF_A), pl.ds(part[1] * HALF_O, HALF_O)]


def window_part(ref, part):
    return ref.at[pl.ds((1 - part[0]) * HALF_A, HALF_A), pl.ds((1 - part[1]) * HALF_O, HALF_O)]


def remote(src, dst, send_sem, recv_sem, device):
    return pltpu.make_async_remote_copy(
        src_ref=src, dst_ref=dst, send_sem=send_sem, recv_sem=recv_sem, device_id=device, device_id_type=MESH
    )


def dot(a, b):
    return jnp.dot(a, b, preferred_element_type=F32)


def dot_nt(a, b):
    return lax.dot_general(a, b, (((1,), (1,)), ((), ())), preferred_element_type=F32)


def dot_tn(a, b):
    return lax.dot_general(a, b, (((0,), (0,)), ((), ())), preferred_element_type=F32)


def spread(block_ref, wide):
    def step(r, _):
        for c in range(WO // 2):
            pair = jnp.concatenate((block_ref[r, 2 * c].astype(F32), block_ref[r, 2 * c + 1].astype(F32)), axis=0)
            at = pl.multiple_of(24 * r + 8 * c, 8)
            for j in range(D // 128):
                wide[j, pl.ds(at, 8), :] = pair[:, 128 * j : 128 * j + 128]
        return 0

    lax.fori_loop(0, WA, step, 0, unroll=2)


def gather(wide, block_ref):
    def step(r, _):
        for c in range(WO // 2):
            at = pl.multiple_of(24 * r + 8 * c, 8)
            pair = jnp.concatenate([wide[j, pl.ds(at, 8), :] for j in range(D // 128)], axis=1)
            block_ref[r, 2 * c] = pair[:LEV].astype(BF16)
            block_ref[r, 2 * c + 1] = pair[LEV:].astype(BF16)
        return 0

    lax.fori_loop(0, WA, step, 0, unroll=2)


def load_level(wide, level):
    return jnp.concatenate([wide[j, pl.ds(level, CELLS, stride=LEV), :] for j in range(D // 128)], axis=1)


def store_level(wide, level, value):
    for j in range(D // 128):
        wide[j, pl.ds(level, CELLS, stride=LEV), :] = value[:, 128 * j : 128 * j + 128]


def rows_of(level):
    return pl.ds(level * CELLS, CELLS)


def window_masks(ids, same):
    labels = jnp.zeros((LEV, 128), F32)
    for c in range(WO):
        row = lax.broadcasted_iota(jnp.int32, (WA, 128), 0)
        cell = lax.broadcasted_iota(jnp.int32, (WA, 128), 1)
        place_of = jnp.where(cell == WO * row + c, 1.0, 0.0)
        labels = labels + dot(ids[c].astype(F32), place_of)
    for w in range(2):
        row = jnp.broadcast_to(labels[2 * w : 2 * w + 1, :], (128, 128))
        one = (row == row.T)[:CELLS, :CELLS].astype(F32)
        two = jnp.concatenate((one, one), axis=1)
        same[w] = jnp.concatenate((two, two), axis=0)


def head_pair(w, h, qkv, datt, same, att, dqkv):
    low = lax.broadcasted_iota(jnp.int32, (1, 128), 1) < HSZ
    rows = pl.ds(w * SPAN, SPAN)
    at = h * 128
    q2 = qkv[rows, pl.ds(at, 128)]
    k2 = qkv[rows, pl.ds(ATT + at, 128)]
    v2 = qkv[rows, pl.ds(2 * ATT + at, 128)]
    o2 = datt[rows, pl.ds(at, 128)]
    apart = []
    for keep in (low, jnp.logical_not(low)):
        keep_w = jnp.broadcast_to(keep, (SPAN, 128))
        qh = jnp.where(keep_w, q2.astype(F32) * (HSZ**-0.5), 0.0).astype(BF16)
        oh = jnp.where(keep_w, o2.astype(F32), 0.0).astype(BF16)
        scores = jnp.where(same[w] > 0.5, dot_nt(k2, qh), -1e30)
        scores = scores - jnp.max(scores, axis=0, keepdims=True)
        weight = jnp.exp(scores)
        prob = weight * (1.0 / jnp.sum(weight, axis=0, keepdims=True))
        prob_b = prob.astype(BF16)
        d_prob = dot_nt(v2, oh)
        inner = jnp.sum(prob * d_prob, axis=0, keepdims=True)
        d_score = (prob * (d_prob - inner) * (HSZ**-0.5)).astype(BF16)
        apart.append((dot_tn(prob_b, v2), dot_tn(d_score, k2), dot(d_score, q2), dot(prob_b, o2)))
    both = [jnp.where(low, first, second).astype(BF16) for first, second in zip(*apart)]
    att[rows, pl.ds(at, 128)] = both[0]
    dqkv[rows, pl.ds(at, 128)] = both[1]
    dqkv[rows, pl.ds(ATT + at, 128)] = both[2]
    dqkv[rows, pl.ds(2 * ATT + at, 128)] = both[3]


def core_kernel(
    x_ref,
    dy_ref,
    ids_ref,
    gain_ref,
    wqkv_ref,
    wproj_ref,
    y_ref,
    dx_ref,
    qkv_out,
    proj_out,
    gain_out,
    xin,
    dyin,
    xv,
    dyv,
    ids,
    ids_in,
    gain_v,
    wqkv,
    wproj,
    wide,
    xs,
    normed,
    inv,
    hid,
    dys,
    hid_t,
    dys_t,
    qkv,
    datt,
    att,
    dqkv,
    same,
    gbuf,
    r1,
    sx,
    sy,
    r2x,
    r2y,
    tx,
    ty,
    r3,
    u,
    r4,
    load_sem,
    in_send,
    in_recv,
    halo_send,
    halo_recv,
    own_sem,
    send1,
    recv1,
    send2,
    recv2,
    send3,
    recv3,
    send4,
    recv4,
):
    loads = [
        pltpu.make_async_copy(src, dst, load_sem.at[n])
        for n, (src, dst) in enumerate(
            (
                (x_ref, xin),
                (dy_ref, dyin),
                (gain_ref, gain_v),
                (ids_ref, ids_in),
                (wqkv_ref, wqkv),
                (wproj_ref, wproj),
            )
        )
    ]
    for copy in loads:
        copy.start()

    lat, lon, dp = place()
    y_hi, z = lat // 8, lax.rem(lat, 8)
    y_lo, chip_core = lon // 2, lax.rem(lon, 2)
    y_pos = 2 * y_hi + y_lo
    pair = (lat, y_lo * 2 + 1 - chip_core, dp)
    along_x = [lax.rem(dp + k, 4) for k in range(1, 4)]
    x_devices = [(lat, lon, other) for other in along_x]
    along_y = []
    for k in range(1, 4):
        other = lax.rem(y_pos + k, 4)
        along_y.append((other // 2, lax.rem(other, 2)))
    y_devices = [(hi * 8 + z, lo * 2 + chip_core, dp) for hi, lo in along_y]
    along_z = [lax.rem(z + k, 8) for k in range(1, 8)]
    z_devices = [(y_hi * 8 + other, lon, dp) for other in along_z]
    odd, to, source, sent, taken, own = partners()
    barrier = pltpu.get_barrier_semaphore()
    for device in to + source + [pair] + x_devices + y_devices + z_devices:
        pl.semaphore_signal(barrier, inc=1, device_id=device, device_id_type=MESH)

    for n in (0, 1, 3):
        loads[n].wait()
    pl.semaphore_wait(barrier, 3 + 3 + 1 + 3 + 3 + 7)
    arriving = [[], []]
    for n, (src, dst) in enumerate(((xin, xv), (dyin, dyv))):
        for k in range(3):
            sems = (in_send.at[3 * n + k], in_recv.at[3 * n + k])
            arriving[n].append(remote(block_part(src, sent[k]), window_part(dst, sent[k]), *sems, to[k]))
        arriving[n].append(pltpu.make_async_copy(block_part(src, own), window_part(dst, own), own_sem.at[n]))
        send_all(arriving[n])

    @pl.when(odd == 1)
    def _():
        labels = remote(ids_in, ids, in_send.at[6], in_recv.at[6], to[0])
        labels.start()
        labels.wait()

    @pl.when(odd == 0)
    def _():
        labels = pltpu.make_async_copy(ids_in, ids, own_sem.at[2])
        labels.start()
        labels.wait()

    window_masks(ids, same)
    loads[2].wait()
    wait_all(arriving[0])
    gain = gain_v[...]
    spread(xv, wide)
    for level in range(LEV):
        x = load_level(wide, level)
        centred = x - jnp.mean(x, axis=-1, keepdims=True)
        inv_std = lax.rsqrt(jnp.mean(centred * centred, axis=-1, keepdims=True) + 1e-05)
        unit = centred * inv_std
        xs[rows_of(level), :] = x
        normed[rows_of(level), :] = unit
        inv[rows_of(level), :] = jnp.broadcast_to(inv_std, (CELLS, 128))
        hid[rows_of(level), :] = (unit * gain).astype(BF16)
    wait_all(arriving[1])
    spread(dyv, wide)
    for level in range(LEV):
        dys[rows_of(level), :] = load_level(wide, level).astype(BF16)
    loads[4].wait()
    qkv[...] = dot(hid[...], wqkv[...]).astype(BF16)
    loads[5].wait()
    datt[...] = dot_nt(dys[...], wproj[...]).astype(BF16)
    hid_t[...] = hid[...].T
    dys_t[...] = dys[...].T

    def attend(h):
        for w in range(2):
            head_pair(w, h, qkv, datt, same, att, dqkv)

    def grad_chunk(h):
        at = h * 128
        left = jnp.concatenate([dqkv[:, n * ATT + at : n * ATT + at + 128] for n in range(3)], axis=1)
        right = att[:, at : at + 128]

        for n in range(2):
            rows = pl.ds(512 * n, 512)
            part = jnp.concatenate((dot(hid_t[rows, :], left), dot(dys_t[rows, :], right)), axis=1)
            gbuf[h, 8 * n : 8 * n + 8] = part.astype(BF16).reshape(8, 2, 2, 16, WIDE)

    def send_pair(h):
        copy = remote(gbuf.at[h, :, :, 1 - chip_core], r1.at[h], send1.at[h], recv1.at[h], pair)
        copy.start()
        return [copy]

    def add_pair(h):
        s = h // 2

        def step(n, _):
            i, j = n // 2, lax.rem(n, 2)
            total = gbuf[h, i, j, chip_core].astype(F32) + r1[h, i, j].astype(F32)
            if h % 2 == 0:
                for k in range(4):
                    sx[s, k, i // 8, lax.rem(i, 8), j] = total[4 * k : 4 * k + 4].astype(BF16)
            else:
                sy[s, i // 8, lax.rem(i, 8), j] = total.astype(BF16)
            return 0

        lax.fori_loop(0, 32, step, 0, unroll=2)
        copies = []
        for k in range(3):
            sems = (send2.at[h, k], recv2.at[h, k])
            if h % 2 == 0:
                copies.append(remote(sx.at[s, along_x[k]], r2x.at[s, k], *sems, x_devices[k]))
            else:
                hi, lo = along_y[k]
                copies.append(remote(sy.at[s, hi, :, lo], r2y.at[s, k], *sems, y_devices[k]))
        return send_all(copies)

    def add_second(h):
        s = h // 2
        if h % 2 == 0:

            def step(n, _):
                hi, i, j = n // 16, lax.rem(n // 2, 8), lax.rem(n, 2)
                total = sx[s, dp, hi, i, j].astype(F32)
                for k in range(3):
                    total = total + r2x[s, k, hi, i, j].astype(F32)
                tx[s, hi, i, j] = total.astype(BF16)
                return 0

            lax.fori_loop(0, 32, step, 0, unroll=2)
        else:

            def step(i, _):
                total = sy[s, y_hi, i, y_lo].astype(F32)
                for k in range(3):
                    total = total + r2y[s, k, i].astype(F32)
                for k in range(4):
                    ty[s, k, i] = total[4 * k : 4 * k + 4].astype(BF16)
                return 0

            lax.fori_loop(0, 8, step, 0, unroll=2)
        copies = []
        for k in range(3):
            sems = (send3.at[h, k], recv3.at[h, k])
            if h % 2 == 0:
                hi, lo = along_y[k]
                copies.append(remote(tx.at[s, hi, :, lo], r3.at[h, k], *sems, y_devices[k]))
            else:
                copies.append(remote(ty.at[s, along_x[k]], r3.at[h, k], *sems, x_devices[k]))
        return send_all(copies)

    def add_third(h):
        s = h // 2

        def step(i, _):
            total = (tx[s, y_hi, i, y_lo] if h % 2 == 0 else ty[s, dp, i]).astype(F32)
            for k in range(3):
                total = total + r3[h, k, i].astype(F32)
            u[i, :, WIDE * h : WIDE * h + WIDE] = total.astype(BF16)
            return 0

        lax.fori_loop(0, 8, step, 0, unroll=2)

    def send_last():
        return send_all(
            [remote(u.at[along_z[k]], r4.at[k], send4.at[k], recv4.at[k], z_devices[k]) for k in range(7)]
        )

    def add_last():
        total = u[z].astype(F32)
        for k in range(7):
            total = total + r4[k].astype(F32)
        total = total * (1.0 / math.sqrt(73728))
        for h in range(CHUNKS):
            for n in range(3):
                at = WIDE * h + 128 * n
                qkv_out[:, n * ATT + 128 * h : n * ATT + 128 * h + 128] = total[:, at : at + 128]
            proj_out[:, 128 * h : 128 * h + 128] = total[:, WIDE * h + 384 : WIDE * h + 512]

    def send_back(n, src, dst):
        copies = [
            remote(
                window_part(src, taken[k]),
                block_part(dst, taken[k]),
                halo_send.at[3 * n + k],
                halo_recv.at[3 * n + k],
                source[k],
            )
            for k in range(3)
        ]
        copies.append(pltpu.make_async_copy(window_part(src, own), block_part(dst, own), own_sem.at[3 + n]))
        return send_all(copies)

    first, second, third = [None] * 4, [None] * 4, [None] * 4
    for h in range(CHUNKS):
        attend(h)
        grad_chunk(h)
        first[h] = send_pair(h)
        if h > 0:
            wait_all(first[h - 1])
            second[h - 1] = add_pair(h - 1)

    xs[...] += dot(att[...], wproj[...])
    wait_all(first[3])
    second[3] = add_pair(3)
    for level in range(LEV):
        store_level(wide, level, xs[rows_of(level), :])
    gather(wide, xv)
    back = send_back(0, xv, y_ref)
    xs[...] = dot_nt(dqkv[...], wqkv[...])
    for level in range(LEV):
        g = xs[rows_of(level), :] * gain
        unit = normed[rows_of(level), :]
        correction = g - jnp.mean(g, axis=-1, keepdims=True) - unit * jnp.mean(g * unit, axis=-1, keepdims=True)
        inv_std = inv[rows_of(level), 0:1]
        store_level(wide, level, dys[rows_of(level), :].astype(F32) + inv_std * correction)
    gather(wide, dyv)
    back += send_back(1, dyv, dx_ref)
    for h in range(CHUNKS):
        wait_all(second[h])
        third[h] = add_second(h)
    for h in range(CHUNKS):
        wait_all(third[h])
        add_third(h)
    fourth = send_last()
    wait_all(fourth)
    add_last()

    group = lat * 4 + lon
    block = wqkv[pl.ds(pl.multiple_of(16 * group, 16), 16), :].astype(F32)
    w_rows = jnp.zeros((4, QKV), F32)
    for k in range(4):
        w_rows = w_rows + jnp.where(dp == k, block[4 * k : 4 * k + 4], 0.0)
    summed = jnp.sum(w_rows * qkv_out[...], axis=-1, keepdims=True)
    lanes = lax.broadcasted_iota(jnp.int32, (4, 128), 1)
    rows = lax.broadcasted_iota(jnp.int32, (4, 128), 0)
    near = gain_v[:, pl.ds(pl.multiple_of(128 * (group // 8), 128), 128)]
    at = lax.rem(group, 8) * 16 + dp * 4
    gains = jnp.sum(jnp.where(lanes == at + rows, jnp.broadcast_to(near, (4, 128)), 0.0), axis=-1, keepdims=True)
    ratio = jnp.broadcast_to(summed / gains, (4, 128))
    gain_out[...] = jnp.sum(jnp.where(lanes == rows, ratio, 0.0), axis=0, keepdims=True)
    wait_all(back)


def send_all(copies):
    for copy in copies:
        copy.start()
    return copies


def wait_all(copies):
    for copy in copies:
        copy.wait()


def core(x, dy, ids, gain, w_qkv, w_proj):
    block = jax.ShapeDtypeStruct((WA, WO, LEV, D), BF16)
    any_space = pl.BlockSpec(memory_space=pl.ANY)
    vmem = pl.BlockSpec(memory_space=pltpu.VMEM)
    dma = pltpu.SemaphoreType.DMA
    return pl.pallas_call(
        core_kernel,
        out_shape=(
            block,
            block,
            jax.ShapeDtypeStruct((4, QKV), F32),
            jax.ShapeDtypeStruct((4, ATT), F32),
            jax.ShapeDtypeStruct((1, 128), F32),
        ),
        in_specs=[any_space] * 6,
        out_specs=(any_space, any_space, vmem, vmem, vmem),
        scratch_shapes=[
            pltpu.VMEM((WA, WO, LEV, D), BF16),
            pltpu.VMEM((WA, WO, LEV, D), BF16),
            pltpu.VMEM((WA, WO, LEV, D), BF16),
            pltpu.VMEM((WA, WO, LEV, D), BF16),
            pltpu.VMEM((WO, LEV, WA), jnp.int32),
            pltpu.VMEM((WO, LEV, WA), jnp.int32),
            pltpu.VMEM((1, D), F32),
            pltpu.VMEM((D, QKV), BF16),
            pltpu.VMEM((ATT, D), BF16),
            pltpu.VMEM((D // 128, ROWS, 128), F32),
            pltpu.VMEM((ROWS, D), F32),
            pltpu.VMEM((ROWS, D), F32),
            pltpu.VMEM((ROWS, 128), F32),
            pltpu.VMEM((ROWS, D), BF16),
            pltpu.VMEM((ROWS, D), BF16),
            pltpu.VMEM((D, ROWS), BF16),
            pltpu.VMEM((D, ROWS), BF16),
            pltpu.VMEM((ROWS, QKV), BF16),
            pltpu.VMEM((ROWS, ATT), BF16),
            pltpu.VMEM((ROWS, ATT), BF16),
            pltpu.VMEM((ROWS, QKV), BF16),
            pltpu.VMEM((2, SPAN, SPAN), F32),
            pltpu.VMEM((4, 16, 2, 2, 16, WIDE), BF16),
            pltpu.VMEM((4, 16, 2, 16, WIDE), BF16),
            pltpu.VMEM((2, 4, 2, 8, 2, 4, WIDE), BF16),
            pltpu.VMEM((2, 2, 8, 2, 16, WIDE), BF16),
            pltpu.VMEM((2, 3, 2, 8, 2, 4, WIDE), BF16),
            pltpu.VMEM((2, 3, 8, 16, WIDE), BF16),
            pltpu.VMEM((2, 2, 8, 2, 4, WIDE), BF16),
            pltpu.VMEM((2, 4, 8, 4, WIDE), BF16),
            pltpu.VMEM((4, 3, 8, 4, WIDE), BF16),
            pltpu.VMEM((8, 4, COLS), BF16),
            pltpu.VMEM((7, 4, COLS), BF16),
            dma((6,)),
            dma((7,)),
            dma((7,)),
            dma((6,)),
            dma((6,)),
            dma((5,)),
            dma((4,)),
            dma((4,)),
            dma((4, 3)),
            dma((4, 3)),
            dma((4, 3)),
            dma((4, 3)),
            dma((7,)),
            dma((7,)),
        ],
        compiler_params=pltpu.CompilerParams(
            collective_id=1, has_side_effects=True, vmem_limit_bytes=56 * 2**20
        ),
        name="window_attention",
    )(x, dy, ids, gain, w_qkv, w_proj)


def finish_kernel(*refs):
    arrays, results, held, (sems,) = refs[:5], refs[5:10], refs[10:15], refs[15:]
    taken = send_all([pltpu.make_async_copy(arrays[n], held[n], sems.at[n]) for n in range(5)])
    put = []
    for n in range(4):
        taken[n].wait()
        put += send_all([pltpu.make_async_copy(held[n], results[n], sems.at[5 + n])])
    taken[4].wait()
    results[4][...] = held[4][:, :4]
    wait_all(put)


def finish(*arrays):
    any_space = pl.BlockSpec(memory_space=pl.ANY)
    shapes = [jax.ShapeDtypeStruct(a.shape, a.dtype) for a in arrays[:4]] + [jax.ShapeDtypeStruct((1, 4), F32)]
    return pl.pallas_call(
        finish_kernel,
        out_shape=tuple(shapes),
        in_specs=[any_space] * 5,
        out_specs=(any_space,) * 4 + (pl.BlockSpec(memory_space=pltpu.VMEM),),
        scratch_shapes=[pltpu.VMEM(a.shape, a.dtype) for a in arrays] + [pltpu.SemaphoreType.DMA((9,))],
        compiler_params=pltpu.CompilerParams(vmem_limit_bytes=56 * 2**20),
        name="results",
    )(*arrays)


def cells_first(block):
    return block.transpose(0, 2, 3, 1, 4).reshape(WA, WO, LEV, D)


def on_device(inputs, cotangent, gain, w_qkv, w_proj, window_ids):
    y, dx, qkv_part, proj_part, gain_part = core(
        cells_first(inputs),
        cells_first(cotangent),
        window_ids.transpose(2, 0, 1),
        gain.reshape(1, D),
        w_qkv,
        w_proj,
    )
    y, dx, qkv_part, proj_part, gain_part = finish(y, dx, qkv_part, proj_part, gain_part)
    back = lambda block: block[None].transpose(0, 3, 1, 2, 4)
    return back(y), back(dx), qkv_part, proj_part.T, gain_part.reshape(4)


def solution(mesh):
    return jax.shard_map(
        on_device,
        mesh=mesh,
        in_specs=(
            P("dp", None, "lat", "lon", None),
            P("dp", None, "lat", "lon", None),
            P(),
            P(),
            P(),
            P(None, "lat", "lon"),
        ),
        out_specs=(
            P("dp", None, "lat", "lon", None),
            P("dp", None, "lat", "lon", None),
            P(("lat", "lon", "dp"), None),
            P(None, ("lat", "lon", "dp")),
            P(("lat", "lon", "dp")),
        ),
        check_vma=False,
    )
```

```python
import functools
import math

import jax
import jax.numpy as jnp
from jax import lax
from jax.experimental import pallas as pl
from jax.experimental.pallas import tpu as pltpu
from jax.sharding import PartitionSpec as P

HEADS = 8
HSZ = 64
WA = 12
WO = 6
HALF_A = WA // 2
HALF_O = WO // 2
LEV = 4
CELLS = WA * WO
ROWS = CELLS * LEV
SPAN = 2 * CELLS
D = 1024
QKV = 3 * HEADS * HSZ
ATT = HEADS * HSZ
COLS = QKV + ATT
CHUNKS = HEADS // 2
WIDE = COLS // CHUNKS
FIRST_AXIS = 'xyxx'
SLOT = [FIRST_AXIS[:h].count(FIRST_AXIS[h]) for h in range(CHUNKS)]
MESH = pl.DeviceIdType.MESH
F32 = jnp.float32
BF16 = jnp.bfloat16


def place():
    return lax.axis_index("lat"), lax.axis_index("lon"), lax.axis_index("dp")


def wrap(value, size):
    return lax.rem(value + size, size)


def later(lon):
    return 1 - lax.rem(lon, 2)


def partners():
    lat, lon, dp = place()
    west, east = wrap(lon - 1, 4), wrap(lon + 1, 4)
    here, there = later(lon), later(west)
    to = [(wrap(lat + 2 * here - 1, 16), lon, dp), (lat, west, dp), (wrap(lat + 2 * there - 1, 16), west, dp)]
    other = wrap(lat + 1 - 2 * here, 16)
    source = [(other, lon, dp), (lat, east, dp), (other, east, dp)]
    sent = [(here, 1), (1 - there, 0), (there, 0)]
    taken = [(here, 1), (1 - here, 0), (here, 0)]
    own = (1 - here, 1)
    return here, to, source, sent, taken, own


def block_part(ref, part):
    return ref.at[pl.ds(part[0] * HALF_A, HALF_A), pl.ds(part[1] * HALF_O, HALF_O)]


def window_part(ref, part):
    return ref.at[pl.ds((1 - part[0]) * HALF_A, HALF_A), pl.ds((1 - part[1]) * HALF_O, HALF_O)]


def remote(src, dst, send_sem, recv_sem, device):
    return pltpu.make_async_remote_copy(
        src_ref=src, dst_ref=dst, send_sem=send_sem, recv_sem=recv_sem, device_id=device, device_id_type=MESH
    )


def dot(a, b):
    return jnp.dot(a, b, preferred_element_type=F32)


def dot_nt(a, b):
    return lax.dot_general(a, b, (((1,), (1,)), ((), ())), preferred_element_type=F32)


def dot_tn(a, b):
    return lax.dot_general(a, b, (((0,), (0,)), ((), ())), preferred_element_type=F32)


def spread(block_ref, wide):
    def step(r, _):
        for c in range(WO // 2):
            pair = jnp.concatenate((block_ref[r, 2 * c].astype(F32), block_ref[r, 2 * c + 1].astype(F32)), axis=0)
            at = pl.multiple_of(24 * r + 8 * c, 8)
            for j in range(D // 128):
                wide[j, pl.ds(at, 8), :] = pair[:, 128 * j : 128 * j + 128]
        return 0

    lax.fori_loop(0, WA, step, 0, unroll=2)


def gather(wide, block_ref):
    def step(r, _):
        for c in range(WO // 2):
            at = pl.multiple_of(24 * r + 8 * c, 8)
            pair = jnp.concatenate([wide[j, pl.ds(at, 8), :] for j in range(D // 128)], axis=1)
            block_ref[r, 2 * c] = pair[:LEV].astype(BF16)
            block_ref[r, 2 * c + 1] = pair[LEV:].astype(BF16)
        return 0

    lax.fori_loop(0, WA, step, 0, unroll=2)


def load_level(wide, level):
    return jnp.concatenate([wide[j, pl.ds(level, CELLS, stride=LEV), :] for j in range(D // 128)], axis=1)


def store_level(wide, level, value):
    for j in range(D // 128):
        wide[j, pl.ds(level, CELLS, stride=LEV), :] = value[:, 128 * j : 128 * j + 128]


def rows_of(level):
    return pl.ds(level * CELLS, CELLS)


def window_masks(ids, same):
    labels = jnp.zeros((LEV, 128), F32)
    for c in range(WO):
        row = lax.broadcasted_iota(jnp.int32, (WA, 128), 0)
        cell = lax.broadcasted_iota(jnp.int32, (WA, 128), 1)
        place_of = jnp.where(cell == WO * row + c, 1.0, 0.0)
        labels = labels + dot(ids[c].astype(F32), place_of)
    for w in range(2):
        row = jnp.broadcast_to(labels[2 * w : 2 * w + 1, :], (128, 128))
        one = (row == row.T)[:CELLS, :CELLS].astype(F32)
        four = jnp.concatenate((one, one, one, one), axis=1)
        same[w] = jnp.concatenate((four, four), axis=0)


def head_pair(w, h, qkv, datt, same, att, dqkv):
    low = lax.broadcasted_iota(jnp.int32, (1, 128), 1) < HSZ
    rows = pl.ds(w * SPAN, SPAN)
    at = h * 128
    q2 = qkv[rows, pl.ds(at, 128)]
    k2 = qkv[rows, pl.ds(ATT + at, 128)]
    v2 = qkv[rows, pl.ds(2 * ATT + at, 128)]
    o2 = datt[rows, pl.ds(at, 128)]
    low_w = jnp.broadcast_to(low, (SPAN, 128))

    def split(x, scale=1.0):
        x = x.astype(F32) * scale
        return jnp.concatenate((jnp.where(low_w, x, 0.0), jnp.where(low_w, 0.0, x)), axis=0).astype(BF16)

    q4 = split(q2)
    o4 = split(o2)
    scores = jnp.where(same[w] > 0.5, dot_nt(k2, split(q2, HSZ**-0.5)), -1e30)
    scores = scores - jnp.max(scores, axis=0, keepdims=True)
    weight = jnp.exp(scores)
    prob = weight * (1.0 / jnp.sum(weight, axis=0, keepdims=True))
    prob_b = prob.astype(BF16)
    d_prob = dot_nt(v2, o4)
    inner = jnp.sum(prob * d_prob, axis=0, keepdims=True)
    d_score = (prob * (d_prob - inner) * (HSZ**-0.5)).astype(BF16)
    two_att = dot_tn(prob_b, v2)
    two_dq = dot_tn(d_score, k2)
    both = [
        jnp.where(low, two_att[:SPAN], two_att[SPAN:]).astype(BF16),
        jnp.where(low, two_dq[:SPAN], two_dq[SPAN:]).astype(BF16),
        dot(d_score, q4).astype(BF16),
        dot(prob_b, o4).astype(BF16),
    ]
    att[rows, pl.ds(at, 128)] = both[0]
    dqkv[rows, pl.ds(at, 128)] = both[1]
    dqkv[rows, pl.ds(ATT + at, 128)] = both[2]
    dqkv[rows, pl.ds(2 * ATT + at, 128)] = both[3]


def core_kernel(
    x_ref,
    dy_ref,
    ids_ref,
    gain_ref,
    wqkv_ref,
    wproj_ref,
    y_ref,
    dx_ref,
    qkv_out,
    proj_out,
    gain_out,
    xin,
    dyin,
    xv,
    dyv,
    ids,
    ids_in,
    gain_v,
    wqkv,
    wproj,
    wide,
    xs,
    normed,
    inv,
    hid,
    dys,
    hid_t,
    dys_t,
    qkv,
    datt,
    att,
    dqkv,
    same,
    gbuf,
    r1,
    sx,
    sy,
    r2x,
    r2y,
    tx,
    ty,
    r3,
    u,
    r4,
    load_sem,
    in_send,
    in_recv,
    halo_send,
    halo_recv,
    own_sem,
    send1,
    recv1,
    send2,
    recv2,
    send3,
    recv3,
    send4,
    recv4,
):
    loads = [
        pltpu.make_async_copy(src, dst, load_sem.at[n])
        for n, (src, dst) in enumerate(
            (
                (x_ref, xin),
                (dy_ref, dyin),
                (gain_ref, gain_v),
                (ids_ref, ids_in),
                (wqkv_ref, wqkv),
                (wproj_ref, wproj),
            )
        )
    ]
    for copy in loads:
        copy.start()

    lat, lon, dp = place()
    y_hi, z = lat // 8, lax.rem(lat, 8)
    y_lo, chip_core = lon // 2, lax.rem(lon, 2)
    y_pos = 2 * y_hi + y_lo
    pair = (lat, y_lo * 2 + 1 - chip_core, dp)
    along_x = [lax.rem(dp + k, 4) for k in range(1, 4)]
    x_devices = [(lat, lon, other) for other in along_x]
    along_y = []
    for k in range(1, 4):
        other = lax.rem(y_pos + k, 4)
        along_y.append((other // 2, lax.rem(other, 2)))
    y_devices = [(hi * 8 + z, lo * 2 + chip_core, dp) for hi, lo in along_y]
    along_z = [lax.rem(z + k, 8) for k in range(1, 8)]
    z_devices = [(y_hi * 8 + other, lon, dp) for other in along_z]
    odd, to, source, sent, taken, own = partners()
    barrier = pltpu.get_barrier_semaphore()
    for device in to + source + [pair] + x_devices + y_devices + z_devices:
        pl.semaphore_signal(barrier, inc=1, device_id=device, device_id_type=MESH)

    for n in (0, 1, 3):
        loads[n].wait()
    pl.semaphore_wait(barrier, 3 + 3 + 1 + 3 + 3 + 7)
    arriving = [[], []]
    for n, (src, dst) in enumerate(((xin, xv), (dyin, dyv))):
        for k in range(3):
            sems = (in_send.at[3 * n + k], in_recv.at[3 * n + k])
            arriving[n].append(remote(block_part(src, sent[k]), window_part(dst, sent[k]), *sems, to[k]))
        arriving[n].append(pltpu.make_async_copy(block_part(src, own), window_part(dst, own), own_sem.at[n]))
        send_all(arriving[n])

    @pl.when(odd == 1)
    def _():
        labels = remote(ids_in, ids, in_send.at[6], in_recv.at[6], to[0])
        labels.start()
        labels.wait()

    @pl.when(odd == 0)
    def _():
        labels = pltpu.make_async_copy(ids_in, ids, own_sem.at[2])
        labels.start()
        labels.wait()

    window_masks(ids, same)
    loads[2].wait()
    wait_all(arriving[0])
    gain = gain_v[...]
    spread(xv, wide)
    for level in range(LEV):
        x = load_level(wide, level)
        centred = x - jnp.mean(x, axis=-1, keepdims=True)
        inv_std = lax.rsqrt(jnp.mean(centred * centred, axis=-1, keepdims=True) + 1e-05)
        unit = centred * inv_std
        xs[rows_of(level), :] = x
        normed[rows_of(level), :] = unit
        inv[rows_of(level), :] = jnp.broadcast_to(inv_std, (CELLS, 128))
        hid[rows_of(level), :] = (unit * gain).astype(BF16)
    wait_all(arriving[1])
    spread(dyv, wide)
    for level in range(LEV):
        dys[rows_of(level), :] = load_level(wide, level).astype(BF16)
    loads[4].wait()
    qkv[...] = dot(hid[...], wqkv[...]).astype(BF16)
    loads[5].wait()
    datt[...] = dot_nt(dys[...], wproj[...]).astype(BF16)
    hid_t[...] = hid[...].T
    dys_t[...] = dys[...].T

    def attend(h):
        for w in range(2):
            head_pair(w, h, qkv, datt, same, att, dqkv)

    def grad_chunk(h):
        at = h * 128
        left = jnp.concatenate([dqkv[:, n * ATT + at : n * ATT + at + 128] for n in range(3)], axis=1)
        right = att[:, at : at + 128]

        for n in range(2):
            rows = pl.ds(512 * n, 512)
            part = jnp.concatenate((dot(hid_t[rows, :], left), dot(dys_t[rows, :], right)), axis=1)
            gbuf[h, 8 * n : 8 * n + 8] = part.astype(BF16).reshape(8, 2, 2, 16, WIDE)

    def send_pair(h):
        copy = remote(gbuf.at[h, :, :, 1 - chip_core], r1.at[h], send1.at[h], recv1.at[h], pair)
        copy.start()
        return [copy]

    def add_pair(h):
        s = SLOT[h]

        def step(n, _):
            i, j = n // 2, lax.rem(n, 2)
            total = gbuf[h, i, j, chip_core] + r1[h, i, j]
            if FIRST_AXIS[h] == 'x':
                for k in range(4):
                    sx[s, k, i // 8, lax.rem(i, 8), j] = total[4 * k : 4 * k + 4]
            else:
                sy[s, i // 8, lax.rem(i, 8), j] = total
            return 0

        lax.fori_loop(0, 32, step, 0, unroll=2)
        copies = []
        for k in range(3):
            sems = (send2.at[h, k], recv2.at[h, k])
            if FIRST_AXIS[h] == 'x':
                copies.append(remote(sx.at[s, along_x[k]], r2x.at[s, k], *sems, x_devices[k]))
            else:
                hi, lo = along_y[k]
                copies.append(remote(sy.at[s, hi, :, lo], r2y.at[s, k], *sems, y_devices[k]))
        return send_all(copies)

    def add_second(h):
        s = SLOT[h]
        if FIRST_AXIS[h] == 'x':

            def step(n, _):
                hi, i, j = n // 16, lax.rem(n // 2, 8), lax.rem(n, 2)
                total = sx[s, dp, hi, i, j].astype(F32)
                for k in range(3):
                    total = total + r2x[s, k, hi, i, j].astype(F32)
                tx[s, hi, i, j] = total.astype(BF16)
                return 0

            lax.fori_loop(0, 32, step, 0, unroll=2)
        else:

            def step(i, _):
                total = sy[s, y_hi, i, y_lo].astype(F32)
                for k in range(3):
                    total = total + r2y[s, k, i].astype(F32)
                for k in range(4):
                    ty[s, k, i] = total[4 * k : 4 * k + 4].astype(BF16)
                return 0

            lax.fori_loop(0, 8, step, 0, unroll=2)
        copies = []
        for k in range(3):
            sems = (send3.at[h, k], recv3.at[h, k])
            if FIRST_AXIS[h] == 'x':
                hi, lo = along_y[k]
                copies.append(remote(tx.at[s, hi, :, lo], r3.at[h, k], *sems, y_devices[k]))
            else:
                copies.append(remote(ty.at[s, along_x[k]], r3.at[h, k], *sems, x_devices[k]))
        return send_all(copies)

    def add_third(h):
        s = SLOT[h]

        def step(i, _):
            total = (tx[s, y_hi, i, y_lo] if FIRST_AXIS[h] == 'x' else ty[s, dp, i]).astype(F32)
            for k in range(3):
                total = total + r3[h, k, i].astype(F32)
            u[i, :, WIDE * h : WIDE * h + WIDE] = total.astype(BF16)
            return 0

        lax.fori_loop(0, 8, step, 0, unroll=2)

    def send_last():
        return send_all(
            [remote(u.at[along_z[k]], r4.at[k], send4.at[k], recv4.at[k], z_devices[k]) for k in range(7)]
        )

    def add_last():
        total = u[z].astype(F32)
        for k in range(7):
            total = total + r4[k].astype(F32)
        total = total * (1.0 / math.sqrt(73728))
        for h in range(CHUNKS):
            for n in range(3):
                at = WIDE * h + 128 * n
                qkv_out[:, n * ATT + 128 * h : n * ATT + 128 * h + 128] = total[:, at : at + 128]
            proj_out[:, 128 * h : 128 * h + 128] = total[:, WIDE * h + 384 : WIDE * h + 512]

    def send_back(n, src, dst):
        copies = [
            remote(
                window_part(src, taken[k]),
                block_part(dst, taken[k]),
                halo_send.at[3 * n + k],
                halo_recv.at[3 * n + k],
                source[k],
            )
            for k in range(3)
        ]
        copies.append(pltpu.make_async_copy(window_part(src, own), block_part(dst, own), own_sem.at[3 + n]))
        return send_all(copies)

    first, second, third = [None] * 4, [None] * 4, [None] * 4
    for h in range(CHUNKS):
        attend(h)
        if h > 0:
            wait_all(first[h - 1])
            second[h - 1] = add_pair(h - 1)
        grad_chunk(h)
        first[h] = send_pair(h)

    xs[...] += dot(att[...], wproj[...])
    wait_all(first[3])
    second[3] = add_pair(3)
    for level in range(LEV):
        store_level(wide, level, xs[rows_of(level), :])
    gather(wide, xv)
    back = send_back(0, xv, y_ref)
    xs[...] = dot_nt(dqkv[...], wqkv[...])
    for level in range(LEV):
        g = xs[rows_of(level), :] * gain
        unit = normed[rows_of(level), :]
        correction = g - jnp.mean(g, axis=-1, keepdims=True) - unit * jnp.mean(g * unit, axis=-1, keepdims=True)
        inv_std = inv[rows_of(level), 0:1]
        store_level(wide, level, dys[rows_of(level), :].astype(F32) + inv_std * correction)
    gather(wide, dyv)
    back += send_back(1, dyv, dx_ref)
    for h in range(CHUNKS):
        wait_all(second[h])
        third[h] = add_second(h)
    for h in range(CHUNKS):
        wait_all(third[h])
        add_third(h)
    fourth = send_last()
    wait_all(fourth)
    add_last()

    group = lat * 4 + lon
    block = wqkv[pl.ds(pl.multiple_of(16 * group, 16), 16), :].astype(F32)
    w_rows = jnp.zeros((4, QKV), F32)
    for k in range(4):
        w_rows = w_rows + jnp.where(dp == k, block[4 * k : 4 * k + 4], 0.0)
    summed = jnp.sum(w_rows * qkv_out[...], axis=-1, keepdims=True)
    lanes = lax.broadcasted_iota(jnp.int32, (4, 128), 1)
    rows = lax.broadcasted_iota(jnp.int32, (4, 128), 0)
    near = gain_v[:, pl.ds(pl.multiple_of(128 * (group // 8), 128), 128)]
    at = lax.rem(group, 8) * 16 + dp * 4
    gains = jnp.sum(jnp.where(lanes == at + rows, jnp.broadcast_to(near, (4, 128)), 0.0), axis=-1, keepdims=True)
    ratio = jnp.broadcast_to(summed / gains, (4, 128))
    gain_out[...] = jnp.sum(jnp.where(lanes == rows, ratio, 0.0), axis=0, keepdims=True)
    wait_all(back)


def send_all(copies):
    for copy in copies:
        copy.start()
    return copies


def wait_all(copies):
    for copy in copies:
        copy.wait()


def core(x, dy, ids, gain, w_qkv, w_proj):
    block = jax.ShapeDtypeStruct((WA, WO, LEV, D), BF16)
    any_space = pl.BlockSpec(memory_space=pl.ANY)
    vmem = pl.BlockSpec(memory_space=pltpu.VMEM)
    dma = pltpu.SemaphoreType.DMA
    return pl.pallas_call(
        core_kernel,
        out_shape=(
            block,
            block,
            jax.ShapeDtypeStruct((4, QKV), F32),
            jax.ShapeDtypeStruct((4, ATT), F32),
            jax.ShapeDtypeStruct((1, 128), F32),
        ),
        in_specs=[any_space] * 6,
        out_specs=(any_space, any_space, vmem, vmem, vmem),
        scratch_shapes=[
            pltpu.VMEM((WA, WO, LEV, D), BF16),
            pltpu.VMEM((WA, WO, LEV, D), BF16),
            pltpu.VMEM((WA, WO, LEV, D), BF16),
            pltpu.VMEM((WA, WO, LEV, D), BF16),
            pltpu.VMEM((WO, LEV, WA), jnp.int32),
            pltpu.VMEM((WO, LEV, WA), jnp.int32),
            pltpu.VMEM((1, D), F32),
            pltpu.VMEM((D, QKV), BF16),
            pltpu.VMEM((ATT, D), BF16),
            pltpu.VMEM((D // 128, ROWS, 128), F32),
            pltpu.VMEM((ROWS, D), F32),
            pltpu.VMEM((ROWS, D), F32),
            pltpu.VMEM((ROWS, 128), F32),
            pltpu.VMEM((ROWS, D), BF16),
            pltpu.VMEM((ROWS, D), BF16),
            pltpu.VMEM((D, ROWS), BF16),
            pltpu.VMEM((D, ROWS), BF16),
            pltpu.VMEM((ROWS, QKV), BF16),
            pltpu.VMEM((ROWS, ATT), BF16),
            pltpu.VMEM((ROWS, ATT), BF16),
            pltpu.VMEM((ROWS, QKV), BF16),
            pltpu.VMEM((2, SPAN, 2 * SPAN), F32),
            pltpu.VMEM((4, 16, 2, 2, 16, WIDE), BF16),
            pltpu.VMEM((4, 16, 2, 16, WIDE), BF16),
            pltpu.VMEM((3, 4, 2, 8, 2, 4, WIDE), BF16),
            pltpu.VMEM((2, 2, 8, 2, 16, WIDE), BF16),
            pltpu.VMEM((3, 3, 2, 8, 2, 4, WIDE), BF16),
            pltpu.VMEM((2, 3, 8, 16, WIDE), BF16),
            pltpu.VMEM((3, 2, 8, 2, 4, WIDE), BF16),
            pltpu.VMEM((2, 4, 8, 4, WIDE), BF16),
            pltpu.VMEM((4, 3, 8, 4, WIDE), BF16),
            pltpu.VMEM((8, 4, COLS), BF16),
            pltpu.VMEM((7, 4, COLS), BF16),
            dma((6,)),
            dma((7,)),
            dma((7,)),
            dma((6,)),
            dma((6,)),
            dma((5,)),
            dma((4,)),
            dma((4,)),
            dma((4, 3)),
            dma((4, 3)),
            dma((4, 3)),
            dma((4, 3)),
            dma((7,)),
            dma((7,)),
        ],
        compiler_params=pltpu.CompilerParams(
            collective_id=1, has_side_effects=True, vmem_limit_bytes=56 * 2**20
        ),
        name="window_attention",
    )(x, dy, ids, gain, w_qkv, w_proj)


def finish_kernel(*refs):
    arrays, results, held, (sems,) = refs[:5], refs[5:10], refs[10:15], refs[15:]
    taken = send_all([pltpu.make_async_copy(arrays[n], held[n], sems.at[n]) for n in range(5)])
    put = []
    for n in range(4):
        taken[n].wait()
        put += send_all([pltpu.make_async_copy(held[n], results[n], sems.at[5 + n])])
    taken[4].wait()
    results[4][...] = held[4][:, :4]
    wait_all(put)


def finish(*arrays):
    any_space = pl.BlockSpec(memory_space=pl.ANY)
    shapes = [jax.ShapeDtypeStruct(a.shape, a.dtype) for a in arrays[:4]] + [jax.ShapeDtypeStruct((1, 4), F32)]
    return pl.pallas_call(
        finish_kernel,
        out_shape=tuple(shapes),
        in_specs=[any_space] * 5,
        out_specs=(any_space,) * 4 + (pl.BlockSpec(memory_space=pltpu.VMEM),),
        scratch_shapes=[pltpu.VMEM(a.shape, a.dtype) for a in arrays] + [pltpu.SemaphoreType.DMA((9,))],
        compiler_params=pltpu.CompilerParams(vmem_limit_bytes=56 * 2**20),
        name="results",
    )(*arrays)


def cells_first(block):
    return block.transpose(0, 2, 3, 1, 4).reshape(WA, WO, LEV, D)


def on_device(inputs, cotangent, gain, w_qkv, w_proj, window_ids):
    y, dx, qkv_part, proj_part, gain_part = core(
        cells_first(inputs),
        cells_first(cotangent),
        window_ids.transpose(2, 0, 1),
        gain.reshape(1, D),
        w_qkv,
        w_proj,
    )
    y, dx, qkv_part, proj_part, gain_part = finish(y, dx, qkv_part, proj_part, gain_part)
    back = lambda block: block[None].transpose(0, 3, 1, 2, 4)
    return back(y), back(dx), qkv_part, proj_part.T, gain_part.reshape(4)


def solution(mesh):
    return jax.shard_map(
        on_device,
        mesh=mesh,
        in_specs=(
            P("dp", None, "lat", "lon", None),
            P("dp", None, "lat", "lon", None),
            P(),
            P(),
            P(),
            P(None, "lat", "lon"),
        ),
        out_specs=(
            P("dp", None, "lat", "lon", None),
            P("dp", None, "lat", "lon", None),
            P(("lat", "lon", "dp"), None),
            P(None, ("lat", "lon", "dp")),
            P(("lat", "lon", "dp")),
        ),
        check_vma=False,
    )
```

```python
import functools
import math

import jax
import jax.numpy as jnp
from jax import lax
from jax.experimental import pallas as pl
from jax.experimental.pallas import tpu as pltpu
from jax.sharding import PartitionSpec as P

HEADS = 8
HSZ = 64
WA = 12
WO = 6
HALF_A = WA // 2
HALF_O = WO // 2
LEV = 4
CELLS = WA * WO
ROWS = CELLS * LEV
SPAN = 2 * CELLS
D = 1024
QKV = 3 * HEADS * HSZ
ATT = HEADS * HSZ
COLS = QKV + ATT
CHUNKS = HEADS // 2
WIDE = COLS // CHUNKS
FIRST_AXIS = 'xyxx'
SLOT = [FIRST_AXIS[:h].count(FIRST_AXIS[h]) for h in range(CHUNKS)]
MESH = pl.DeviceIdType.MESH
F32 = jnp.float32
BF16 = jnp.bfloat16


def place():
    return lax.axis_index("lat"), lax.axis_index("lon"), lax.axis_index("dp")


def wrap(value, size):
    return lax.rem(value + size, size)


def later(lon):
    return 1 - lax.rem(lon, 2)


def partners():
    lat, lon, dp = place()
    west, east = wrap(lon - 1, 4), wrap(lon + 1, 4)
    here, there = later(lon), later(west)
    to = [(wrap(lat + 2 * here - 1, 16), lon, dp), (lat, west, dp), (wrap(lat + 2 * there - 1, 16), west, dp)]
    other = wrap(lat + 1 - 2 * here, 16)
    source = [(other, lon, dp), (lat, east, dp), (other, east, dp)]
    sent = [(here, 1), (1 - there, 0), (there, 0)]
    taken = [(here, 1), (1 - here, 0), (here, 0)]
    own = (1 - here, 1)
    return here, to, source, sent, taken, own


def block_part(ref, part):
    return ref.at[pl.ds(part[0] * HALF_A, HALF_A), pl.ds(part[1] * HALF_O, HALF_O)]


def window_part(ref, part):
    return ref.at[pl.ds((1 - part[0]) * HALF_A, HALF_A), pl.ds((1 - part[1]) * HALF_O, HALF_O)]


def remote(src, dst, send_sem, recv_sem, device):
    return pltpu.make_async_remote_copy(
        src_ref=src, dst_ref=dst, send_sem=send_sem, recv_sem=recv_sem, device_id=device, device_id_type=MESH
    )


def dot(a, b):
    return jnp.dot(a, b, preferred_element_type=F32)


def dot_nt(a, b):
    return lax.dot_general(a, b, (((1,), (1,)), ((), ())), preferred_element_type=F32)


def dot_tn(a, b):
    return lax.dot_general(a, b, (((0,), (0,)), ((), ())), preferred_element_type=F32)


def spread(block_ref, wide):
    def step(r, _):
        for c in range(WO // 2):
            pair = jnp.concatenate((block_ref[r, 2 * c].astype(F32), block_ref[r, 2 * c + 1].astype(F32)), axis=0)
            at = pl.multiple_of(24 * r + 8 * c, 8)
            for j in range(D // 128):
                wide[j, pl.ds(at, 8), :] = pair[:, 128 * j : 128 * j + 128]
        return 0

    lax.fori_loop(0, WA, step, 0, unroll=2)


def gather(wide, block_ref):
    def step(r, _):
        for c in range(WO // 2):
            at = pl.multiple_of(24 * r + 8 * c, 8)
            pair = jnp.concatenate([wide[j, pl.ds(at, 8), :] for j in range(D // 128)], axis=1)
            block_ref[r, 2 * c] = pair[:LEV].astype(BF16)
            block_ref[r, 2 * c + 1] = pair[LEV:].astype(BF16)
        return 0

    lax.fori_loop(0, WA, step, 0, unroll=2)


def load_level(wide, level):
    return jnp.concatenate([wide[j, pl.ds(level, CELLS, stride=LEV), :] for j in range(D // 128)], axis=1)


def store_level(wide, level, value):
    for j in range(D // 128):
        wide[j, pl.ds(level, CELLS, stride=LEV), :] = value[:, 128 * j : 128 * j + 128]


def rows_of(level):
    return pl.ds(level * CELLS, CELLS)


def window_masks(ids, same):
    labels = jnp.zeros((LEV, 128), F32)
    for c in range(WO):
        row = lax.broadcasted_iota(jnp.int32, (WA, 128), 0)
        cell = lax.broadcasted_iota(jnp.int32, (WA, 128), 1)
        place_of = jnp.where(cell == WO * row + c, 1.0, 0.0)
        labels = labels + dot(ids[c].astype(F32), place_of)
    for w in range(2):
        row = jnp.broadcast_to(labels[2 * w : 2 * w + 1, :], (128, 128))
        one = (row == row.T)[:CELLS, :CELLS].astype(F32)
        four = jnp.concatenate((one, one, one, one), axis=1)
        same[w] = jnp.concatenate((four, four), axis=0)


def head_pair(w, h, qkv, datt, same, att, dqkv):
    low = lax.broadcasted_iota(jnp.int32, (1, 128), 1) < HSZ
    rows = pl.ds(w * SPAN, SPAN)
    at = h * 128
    q2 = qkv[rows, pl.ds(at, 128)]
    k2 = qkv[rows, pl.ds(ATT + at, 128)]
    v2 = qkv[rows, pl.ds(2 * ATT + at, 128)]
    o2 = datt[rows, pl.ds(at, 128)]
    low_w = jnp.broadcast_to(low, (SPAN, 128))

    def split(x, scale=1.0):
        x = x.astype(F32) * scale
        return jnp.concatenate((jnp.where(low_w, x, 0.0), jnp.where(low_w, 0.0, x)), axis=0).astype(BF16)

    q4 = split(q2)
    o4 = split(o2)
    scores = jnp.where(same[w] > 0.5, dot_nt(k2, split(q2, HSZ**-0.5)), -1e30)
    scores = scores - jnp.max(scores, axis=0, keepdims=True)
    weight = jnp.exp(scores)
    prob = weight * (1.0 / jnp.sum(weight, axis=0, keepdims=True))
    prob_b = prob.astype(BF16)
    d_prob = dot_nt(v2, o4)
    inner = jnp.sum(prob * d_prob, axis=0, keepdims=True)
    d_score = (prob * (d_prob - inner) * (HSZ**-0.5)).astype(BF16)
    two_att = dot_tn(prob_b, v2)
    two_dq = dot_tn(d_score, k2)
    both = [
        jnp.where(low, two_att[:SPAN], two_att[SPAN:]).astype(BF16),
        jnp.where(low, two_dq[:SPAN], two_dq[SPAN:]).astype(BF16),
        dot(d_score, q4).astype(BF16),
        dot(prob_b, o4).astype(BF16),
    ]
    att[rows, pl.ds(at, 128)] = both[0]
    dqkv[rows, pl.ds(at, 128)] = both[1]
    dqkv[rows, pl.ds(ATT + at, 128)] = both[2]
    dqkv[rows, pl.ds(2 * ATT + at, 128)] = both[3]


def core_kernel(
    x_ref,
    dy_ref,
    ids_ref,
    gain_ref,
    wqkv_ref,
    wproj_ref,
    y_ref,
    dx_ref,
    qkv_out,
    proj_out,
    gain_out,
    xin,
    dyin,
    xv,
    dyv,
    ids,
    ids_in,
    gain_v,
    wqkv,
    wproj,
    wide,
    xs,
    normed,
    inv,
    hid,
    dys,
    hid_t,
    dys_t,
    qkv,
    datt,
    att,
    dqkv,
    same,
    gbuf,
    r1,
    sx,
    sy,
    r2x,
    r2y,
    tx,
    ty,
    r3,
    u,
    r4,
    load_sem,
    in_send,
    in_recv,
    halo_send,
    halo_recv,
    own_sem,
    send1,
    recv1,
    send2,
    recv2,
    send3,
    recv3,
    send4,
    recv4,
):
    loads = [
        pltpu.make_async_copy(src, dst, load_sem.at[n])
        for n, (src, dst) in enumerate(
            (
                (x_ref, xin),
                (dy_ref, dyin),
                (gain_ref, gain_v),
                (ids_ref, ids_in),
                (wqkv_ref, wqkv),
                (wproj_ref, wproj),
            )
        )
    ]
    for copy in loads:
        copy.start()

    lat, lon, dp = place()
    y_hi, z = lat // 8, lax.rem(lat, 8)
    y_lo, chip_core = lon // 2, lax.rem(lon, 2)
    y_pos = 2 * y_hi + y_lo
    pair = (lat, y_lo * 2 + 1 - chip_core, dp)
    along_x = [lax.rem(dp + k, 4) for k in range(1, 4)]
    x_devices = [(lat, lon, other) for other in along_x]
    along_y = []
    for k in range(1, 4):
        other = lax.rem(y_pos + k, 4)
        along_y.append((other // 2, lax.rem(other, 2)))
    y_devices = [(hi * 8 + z, lo * 2 + chip_core, dp) for hi, lo in along_y]
    along_z = [lax.rem(z + k, 8) for k in range(1, 8)]
    z_devices = [(y_hi * 8 + other, lon, dp) for other in along_z]
    odd, to, source, sent, taken, own = partners()
    barrier = pltpu.get_barrier_semaphore()
    for device in to + source + [pair] + x_devices + y_devices + z_devices:
        pl.semaphore_signal(barrier, inc=1, device_id=device, device_id_type=MESH)

    for n in (0, 1, 3):
        loads[n].wait()
    pl.semaphore_wait(barrier, 3 + 3 + 1 + 3 + 3 + 7)
    arriving = [[], []]
    local = []
    for n, (src, dst) in enumerate(((xin, xv), (dyin, dyv))):
        for k in range(3):
            sems = (in_send.at[3 * n + k], in_recv.at[3 * n + k])
            arriving[n].append(remote(block_part(src, sent[k]), window_part(dst, sent[k]), *sems, to[k]))
        local.append(pltpu.make_async_copy(block_part(src, own), window_part(dst, own), own_sem.at[n]))
        send_all(arriving[n] + local[n:])

    @pl.when(odd == 1)
    def _():
        labels = remote(ids_in, ids, in_send.at[6], in_recv.at[6], to[0])
        labels.start()
        labels.wait()

    @pl.when(odd == 0)
    def _():
        labels = pltpu.make_async_copy(ids_in, ids, own_sem.at[2])
        labels.start()
        labels.wait()

    window_masks(ids, same)
    loads[2].wait()
    take_all(arriving[0])
    local[0].wait()
    gain = gain_v[...]
    spread(xv, wide)
    for level in range(LEV):
        x = load_level(wide, level)
        centred = x - jnp.mean(x, axis=-1, keepdims=True)
        inv_std = lax.rsqrt(jnp.mean(centred * centred, axis=-1, keepdims=True) + 1e-05)
        unit = centred * inv_std
        xs[rows_of(level), :] = x
        normed[rows_of(level), :] = unit
        inv[rows_of(level), :] = jnp.broadcast_to(inv_std, (CELLS, 128))
        hid[rows_of(level), :] = (unit * gain).astype(BF16)
    take_all(arriving[1])
    local[1].wait()
    spread(dyv, wide)
    for level in range(LEV):
        dys[rows_of(level), :] = load_level(wide, level).astype(BF16)
    loads[4].wait()
    qkv[...] = dot(hid[...], wqkv[...]).astype(BF16)
    loads[5].wait()
    datt[...] = dot_nt(dys[...], wproj[...]).astype(BF16)
    hid_t[...] = hid[...].T
    dys_t[...] = dys[...].T

    def attend(h):
        for w in range(2):
            head_pair(w, h, qkv, datt, same, att, dqkv)

    def grad_chunk(h):
        at = h * 128
        left = jnp.concatenate([dqkv[:, n * ATT + at : n * ATT + at + 128] for n in range(3)], axis=1)
        right = att[:, at : at + 128]

        for n in range(2):
            rows = pl.ds(512 * n, 512)
            part = jnp.concatenate((dot(hid_t[rows, :], left), dot(dys_t[rows, :], right)), axis=1)
            gbuf[h, 8 * n : 8 * n + 8] = part.astype(BF16).reshape(8, 2, 2, 16, WIDE)

    def send_pair(h):
        copy = remote(gbuf.at[h, :, :, 1 - chip_core], r1.at[h], send1.at[h], recv1.at[h], pair)
        copy.start()
        return [copy]

    def add_pair(h):
        s = SLOT[h]

        def step(n, _):
            i, j = n // 2, lax.rem(n, 2)
            total = gbuf[h, i, j, chip_core] + r1[h, i, j]
            if FIRST_AXIS[h] == 'x':
                for k in range(4):
                    sx[s, k, i // 8, lax.rem(i, 8), j] = total[4 * k : 4 * k + 4]
            else:
                sy[s, i // 8, lax.rem(i, 8), j] = total
            return 0

        lax.fori_loop(0, 32, step, 0, unroll=8)
        copies = []
        for k in range(3):
            sems = (send2.at[h, k], recv2.at[h, k])
            if FIRST_AXIS[h] == 'x':
                copies.append(remote(sx.at[s, along_x[k]], r2x.at[s, k], *sems, x_devices[k]))
            else:
                hi, lo = along_y[k]
                copies.append(remote(sy.at[s, hi, :, lo], r2y.at[s, k], *sems, y_devices[k]))
        return send_all(copies)

    def add_second(h):
        s = SLOT[h]
        if FIRST_AXIS[h] == 'x':

            def step(n, _):
                hi, i, j = n // 16, lax.rem(n // 2, 8), lax.rem(n, 2)
                total = sx[s, dp, hi, i, j].astype(F32)
                for k in range(3):
                    total = total + r2x[s, k, hi, i, j].astype(F32)
                tx[s, hi, i, j] = total.astype(BF16)
                return 0

            lax.fori_loop(0, 32, step, 0, unroll=8)
        else:

            def step(i, _):
                total = sy[s, y_hi, i, y_lo].astype(F32)
                for k in range(3):
                    total = total + r2y[s, k, i].astype(F32)
                for k in range(4):
                    ty[s, k, i] = total[4 * k : 4 * k + 4].astype(BF16)
                return 0

            lax.fori_loop(0, 8, step, 0, unroll=4)
        copies = []
        for k in range(3):
            sems = (send3.at[h, k], recv3.at[h, k])
            if FIRST_AXIS[h] == 'x':
                hi, lo = along_y[k]
                copies.append(remote(tx.at[s, hi, :, lo], r3.at[h, k], *sems, y_devices[k]))
            else:
                copies.append(remote(ty.at[s, along_x[k]], r3.at[h, k], *sems, x_devices[k]))
        return send_all(copies)

    def add_third(h):
        s = SLOT[h]

        def step(i, _):
            total = (tx[s, y_hi, i, y_lo] if FIRST_AXIS[h] == 'x' else ty[s, dp, i]).astype(F32)
            for k in range(3):
                total = total + r3[h, k, i].astype(F32)
            u[i, :, WIDE * h : WIDE * h + WIDE] = total.astype(BF16)
            return 0

        lax.fori_loop(0, 8, step, 0, unroll=4)

    def send_last():
        return send_all(
            [remote(u.at[along_z[k]], r4.at[k], send4.at[k], recv4.at[k], z_devices[k]) for k in range(7)]
        )

    def add_last():
        total = u[z].astype(F32)
        for k in range(7):
            total = total + r4[k].astype(F32)
        total = total * (1.0 / math.sqrt(73728))
        for h in range(CHUNKS):
            for n in range(3):
                at = WIDE * h + 128 * n
                qkv_out[:, n * ATT + 128 * h : n * ATT + 128 * h + 128] = total[:, at : at + 128]
            proj_out[:, 128 * h : 128 * h + 128] = total[:, WIDE * h + 384 : WIDE * h + 512]

    def send_back(n, src, dst):
        copies = [
            remote(
                window_part(src, taken[k]),
                block_part(dst, taken[k]),
                halo_send.at[3 * n + k],
                halo_recv.at[3 * n + k],
                source[k],
            )
            for k in range(3)
        ]
        copies.append(pltpu.make_async_copy(window_part(src, own), block_part(dst, own), own_sem.at[3 + n]))
        return send_all(copies)

    first, second, third = [None] * 4, [None] * 4, [None] * 4
    for h in range(CHUNKS):
        attend(h)
        if h > 0:
            take_all(first[h - 1])
            second[h - 1] = add_pair(h - 1)
        grad_chunk(h)
        first[h] = send_pair(h)

    xs[...] += dot(att[...], wproj[...])
    take_all(first[3])
    second[3] = add_pair(3)
    for level in range(LEV):
        store_level(wide, level, xs[rows_of(level), :])
    gather(wide, xv)
    back = send_back(0, xv, y_ref)
    xs[...] = dot_nt(dqkv[...], wqkv[...])
    for level in range(LEV):
        g = xs[rows_of(level), :] * gain
        unit = normed[rows_of(level), :]
        correction = g - jnp.mean(g, axis=-1, keepdims=True) - unit * jnp.mean(g * unit, axis=-1, keepdims=True)
        inv_std = inv[rows_of(level), 0:1]
        store_level(wide, level, dys[rows_of(level), :].astype(F32) + inv_std * correction)
    gather(wide, dyv)
    back += send_back(1, dyv, dx_ref)
    for h in range(CHUNKS):
        take_all(second[h])
        third[h] = add_second(h)
    for h in range(CHUNKS):
        take_all(third[h])
        add_third(h)
    fourth = send_last()
    group = lat * 4 + lon
    block = wqkv[pl.ds(pl.multiple_of(16 * group, 16), 16), :].astype(F32)
    w_rows = jnp.zeros((4, QKV), F32)
    for k in range(4):
        w_rows = w_rows + jnp.where(dp == k, block[4 * k : 4 * k + 4], 0.0)
    lanes = lax.broadcasted_iota(jnp.int32, (4, 128), 1)
    rows = lax.broadcasted_iota(jnp.int32, (4, 128), 0)
    near = gain_v[:, pl.ds(pl.multiple_of(128 * (group // 8), 128), 128)]
    at = lax.rem(group, 8) * 16 + dp * 4
    gains = jnp.sum(jnp.where(lanes == at + rows, jnp.broadcast_to(near, (4, 128)), 0.0), axis=-1, keepdims=True)
    w_rows = w_rows / gains
    take_all(fourth)
    add_last()

    summed = jnp.broadcast_to(jnp.sum(w_rows * qkv_out[...], axis=-1, keepdims=True), (4, 128))
    gain_out[...] = jnp.sum(jnp.where(lanes == rows, summed, 0.0), axis=0, keepdims=True)
    for copies in arriving + first + second + third + [fourth]:
        for copy in copies:
            copy.wait_send()
    wait_all(back)


def send_all(copies):
    for copy in copies:
        copy.start()
    return copies


def take_all(copies):
    for copy in copies:
        copy.wait_recv()


def wait_all(copies):
    for copy in copies:
        copy.wait()


def core(x, dy, ids, gain, w_qkv, w_proj):
    block = jax.ShapeDtypeStruct((WA, WO, LEV, D), BF16)
    any_space = pl.BlockSpec(memory_space=pl.ANY)
    vmem = pl.BlockSpec(memory_space=pltpu.VMEM)
    dma = pltpu.SemaphoreType.DMA
    return pl.pallas_call(
        core_kernel,
        out_shape=(
            block,
            block,
            jax.ShapeDtypeStruct((4, QKV), F32),
            jax.ShapeDtypeStruct((4, ATT), F32),
            jax.ShapeDtypeStruct((1, 128), F32),
        ),
        in_specs=[any_space] * 6,
        out_specs=(any_space, any_space, vmem, vmem, vmem),
        scratch_shapes=[
            pltpu.VMEM((WA, WO, LEV, D), BF16),
            pltpu.VMEM((WA, WO, LEV, D), BF16),
            pltpu.VMEM((WA, WO, LEV, D), BF16),
            pltpu.VMEM((WA, WO, LEV, D), BF16),
            pltpu.VMEM((WO, LEV, WA), jnp.int32),
            pltpu.VMEM((WO, LEV, WA), jnp.int32),
            pltpu.VMEM((1, D), F32),
            pltpu.VMEM((D, QKV), BF16),
            pltpu.VMEM((ATT, D), BF16),
            pltpu.VMEM((D // 128, ROWS, 128), F32),
            pltpu.VMEM((ROWS, D), F32),
            pltpu.VMEM((ROWS, D), F32),
            pltpu.VMEM((ROWS, 128), F32),
            pltpu.VMEM((ROWS, D), BF16),
            pltpu.VMEM((ROWS, D), BF16),
            pltpu.VMEM((D, ROWS), BF16),
            pltpu.VMEM((D, ROWS), BF16),
            pltpu.VMEM((ROWS, QKV), BF16),
            pltpu.VMEM((ROWS, ATT), BF16),
            pltpu.VMEM((ROWS, ATT), BF16),
            pltpu.VMEM((ROWS, QKV), BF16),
            pltpu.VMEM((2, SPAN, 2 * SPAN), F32),
            pltpu.VMEM((4, 16, 2, 2, 16, WIDE), BF16),
            pltpu.VMEM((4, 16, 2, 16, WIDE), BF16),
            pltpu.VMEM((3, 4, 2, 8, 2, 4, WIDE), BF16),
            pltpu.VMEM((2, 2, 8, 2, 16, WIDE), BF16),
            pltpu.VMEM((3, 3, 2, 8, 2, 4, WIDE), BF16),
            pltpu.VMEM((2, 3, 8, 16, WIDE), BF16),
            pltpu.VMEM((3, 2, 8, 2, 4, WIDE), BF16),
            pltpu.VMEM((2, 4, 8, 4, WIDE), BF16),
            pltpu.VMEM((4, 3, 8, 4, WIDE), BF16),
            pltpu.VMEM((8, 4, COLS), BF16),
            pltpu.VMEM((7, 4, COLS), BF16),
            dma((6,)),
            dma((7,)),
            dma((7,)),
            dma((6,)),
            dma((6,)),
            dma((5,)),
            dma((4,)),
            dma((4,)),
            dma((4, 3)),
            dma((4, 3)),
            dma((4, 3)),
            dma((4, 3)),
            dma((7,)),
            dma((7,)),
        ],
        compiler_params=pltpu.CompilerParams(
            collective_id=1, has_side_effects=True, vmem_limit_bytes=56 * 2**20
        ),
        name="window_attention",
    )(x, dy, ids, gain, w_qkv, w_proj)


def finish_kernel(*refs):
    arrays, results, held, (sems,) = refs[:5], refs[5:10], refs[10:15], refs[15:]
    taken = send_all([pltpu.make_async_copy(arrays[n], held[n], sems.at[n]) for n in range(5)])
    put = []
    for n in range(4):
        taken[n].wait()
        put += send_all([pltpu.make_async_copy(held[n], results[n], sems.at[5 + n])])
    taken[4].wait()
    results[4][...] = held[4][:, :4]
    wait_all(put)


def finish(*arrays):
    any_space = pl.BlockSpec(memory_space=pl.ANY)
    shapes = [jax.ShapeDtypeStruct(a.shape, a.dtype) for a in arrays[:4]] + [jax.ShapeDtypeStruct((1, 4), F32)]
    return pl.pallas_call(
        finish_kernel,
        out_shape=tuple(shapes),
        in_specs=[any_space] * 5,
        out_specs=(any_space,) * 4 + (pl.BlockSpec(memory_space=pltpu.VMEM),),
        scratch_shapes=[pltpu.VMEM(a.shape, a.dtype) for a in arrays] + [pltpu.SemaphoreType.DMA((9,))],
        compiler_params=pltpu.CompilerParams(vmem_limit_bytes=56 * 2**20),
        name="results",
    )(*arrays)


def cells_first(block):
    return block.transpose(0, 2, 3, 1, 4).reshape(WA, WO, LEV, D)


def on_device(inputs, cotangent, gain, w_qkv, w_proj, window_ids):
    y, dx, qkv_part, proj_part, gain_part = core(
        cells_first(inputs),
        cells_first(cotangent),
        window_ids.transpose(2, 0, 1),
        gain.reshape(1, D),
        w_qkv,
        w_proj,
    )
    y, dx, qkv_part, proj_part, gain_part = finish(y, dx, qkv_part, proj_part, gain_part)
    back = lambda block: block[None].transpose(0, 3, 1, 2, 4)
    return back(y), back(dx), qkv_part, proj_part.T, gain_part.reshape(4)


def solution(mesh):
    return jax.shard_map(
        on_device,
        mesh=mesh,
        in_specs=(
            P("dp", None, "lat", "lon", None),
            P("dp", None, "lat", "lon", None),
            P(),
            P(),
            P(),
            P(None, "lat", "lon"),
        ),
        out_specs=(
            P("dp", None, "lat", "lon", None),
            P("dp", None, "lat", "lon", None),
            P(("lat", "lon", "dp"), None),
            P(None, ("lat", "lon", "dp")),
            P(("lat", "lon", "dp")),
        ),
        check_vma=False,
    )
```

```python
import functools
import math

import jax
import jax.numpy as jnp
from jax import lax
from jax.experimental import pallas as pl
from jax.experimental.pallas import tpu as pltpu
from jax.sharding import PartitionSpec as P

HEADS = 8
HSZ = 64
WA = 12
WO = 6
HALF_A = WA // 2
HALF_O = WO // 2
LEV = 4
CELLS = WA * WO
ROWS = CELLS * LEV
SPAN = 2 * CELLS
D = 1024
QKV = 3 * HEADS * HSZ
ATT = HEADS * HSZ
COLS = QKV + ATT
CHUNKS = HEADS // 2
WIDE = COLS // CHUNKS
FIRST_AXIS = 'xyxx'
SLOT = [FIRST_AXIS[:h].count(FIRST_AXIS[h]) for h in range(CHUNKS)]
MESH = pl.DeviceIdType.MESH
F32 = jnp.float32
BF16 = jnp.bfloat16


def place():
    return lax.axis_index("lat"), lax.axis_index("lon"), lax.axis_index("dp")


def wrap(value, size):
    return lax.rem(value + size, size)


def later(lon):
    return 1 - lax.rem(lon, 2)


def partners():
    lat, lon, dp = place()
    west, east = wrap(lon - 1, 4), wrap(lon + 1, 4)
    here, there = later(lon), later(west)
    to = [(wrap(lat + 2 * here - 1, 16), lon, dp), (lat, west, dp), (wrap(lat + 2 * there - 1, 16), west, dp)]
    other = wrap(lat + 1 - 2 * here, 16)
    source = [(other, lon, dp), (lat, east, dp), (other, east, dp)]
    sent = [(here, 1), (1 - there, 0), (there, 0)]
    taken = [(here, 1), (1 - here, 0), (here, 0)]
    own = (1 - here, 1)
    return here, to, source, sent, taken, own


def block_part(ref, part):
    return ref.at[pl.ds(part[0] * HALF_A, HALF_A), pl.ds(part[1] * HALF_O, HALF_O)]


def window_part(ref, part):
    return ref.at[pl.ds((1 - part[0]) * HALF_A, HALF_A), pl.ds((1 - part[1]) * HALF_O, HALF_O)]


def remote(src, dst, send_sem, recv_sem, device):
    return pltpu.make_async_remote_copy(
        src_ref=src, dst_ref=dst, send_sem=send_sem, recv_sem=recv_sem, device_id=device, device_id_type=MESH
    )


def dot(a, b):
    return jnp.dot(a, b, preferred_element_type=F32)


def dot_nt(a, b):
    return lax.dot_general(a, b, (((1,), (1,)), ((), ())), preferred_element_type=F32)


def dot_tn(a, b):
    return lax.dot_general(a, b, (((0,), (0,)), ((), ())), preferred_element_type=F32)


def spread(block_ref, wide):
    def step(r, _):
        for c in range(WO // 2):
            pair = jnp.concatenate((block_ref[r, 2 * c].astype(F32), block_ref[r, 2 * c + 1].astype(F32)), axis=0)
            at = pl.multiple_of(24 * r + 8 * c, 8)
            for j in range(D // 128):
                wide[j, pl.ds(at, 8), :] = pair[:, 128 * j : 128 * j + 128]
        return 0

    lax.fori_loop(0, WA, step, 0, unroll=2)


def gather(wide, block_ref):
    def step(r, _):
        for c in range(WO // 2):
            at = pl.multiple_of(24 * r + 8 * c, 8)
            pair = jnp.concatenate([wide[j, pl.ds(at, 8), :] for j in range(D // 128)], axis=1)
            block_ref[r, 2 * c] = pair[:LEV].astype(BF16)
            block_ref[r, 2 * c + 1] = pair[LEV:].astype(BF16)
        return 0

    lax.fori_loop(0, WA, step, 0, unroll=2)


def load_level(wide, level):
    return jnp.concatenate([wide[j, pl.ds(level, CELLS, stride=LEV), :] for j in range(D // 128)], axis=1)


def store_level(wide, level, value):
    for j in range(D // 128):
        wide[j, pl.ds(level, CELLS, stride=LEV), :] = value[:, 128 * j : 128 * j + 128]


def rows_of(level):
    return pl.ds(level * CELLS, CELLS)


def window_masks(ids, same):
    labels = jnp.zeros((LEV, 128), F32)
    for c in range(WO):
        row = lax.broadcasted_iota(jnp.int32, (WA, 128), 0)
        cell = lax.broadcasted_iota(jnp.int32, (WA, 128), 1)
        place_of = jnp.where(cell == WO * row + c, 1.0, 0.0)
        labels = labels + dot(ids[c].astype(F32), place_of)
    for w in range(2):
        row = jnp.broadcast_to(labels[2 * w : 2 * w + 1, :], (128, 128))
        one = (row == row.T)[:CELLS, :CELLS].astype(F32)
        four = jnp.concatenate((one, one, one, one), axis=1)
        same[w] = jnp.concatenate((four, four), axis=0)


def head_pair(w, h, qkv, datt, same, att, dqkv):
    low = lax.broadcasted_iota(jnp.int32, (1, 128), 1) < HSZ
    rows = pl.ds(w * SPAN, SPAN)
    at = h * 128
    q2 = qkv[rows, pl.ds(at, 128)]
    k2 = qkv[rows, pl.ds(ATT + at, 128)]
    v2 = qkv[rows, pl.ds(2 * ATT + at, 128)]
    o2 = datt[rows, pl.ds(at, 128)]
    low_w = jnp.broadcast_to(low, (SPAN, 128))

    def split(x, scale=1.0):
        x = x.astype(F32) * scale
        return jnp.concatenate((jnp.where(low_w, x, 0.0), jnp.where(low_w, 0.0, x)), axis=0).astype(BF16)

    q4 = split(q2)
    o4 = split(o2)
    scores = jnp.where(same[w] > 0.5, dot_nt(k2, split(q2, HSZ**-0.5)), -1e30)
    scores = scores - jnp.max(scores, axis=0, keepdims=True)
    weight = jnp.exp(scores)
    prob = weight * (1.0 / jnp.sum(weight, axis=0, keepdims=True))
    prob_b = prob.astype(BF16)
    d_prob = dot_nt(v2, o4)
    inner = jnp.sum(prob * d_prob, axis=0, keepdims=True)
    d_score = (prob * (d_prob - inner) * (HSZ**-0.5)).astype(BF16)
    two_att = dot_tn(prob_b, v2)
    two_dq = dot_tn(d_score, k2)
    both = [
        jnp.where(low, two_att[:SPAN], two_att[SPAN:]).astype(BF16),
        jnp.where(low, two_dq[:SPAN], two_dq[SPAN:]).astype(BF16),
        dot(d_score, q4).astype(BF16),
        dot(prob_b, o4).astype(BF16),
    ]
    att[rows, pl.ds(at, 128)] = both[0]
    dqkv[rows, pl.ds(at, 128)] = both[1]
    dqkv[rows, pl.ds(ATT + at, 128)] = both[2]
    dqkv[rows, pl.ds(2 * ATT + at, 128)] = both[3]


def core_kernel(
    x_ref,
    dy_ref,
    ids_ref,
    gain_ref,
    wqkv_ref,
    wproj_ref,
    y_ref,
    dx_ref,
    qkv_out,
    proj_out,
    gain_out,
    xin,
    dyin,
    xv,
    dyv,
    ids,
    ids_in,
    gain_v,
    wqkv,
    wproj,
    wide,
    xs,
    normed,
    inv,
    hid,
    dys,
    hid_t,
    dys_t,
    qkv,
    datt,
    att,
    dqkv,
    same,
    gbuf,
    r1,
    sx,
    sy,
    r2x,
    r2y,
    tx,
    ty,
    r3,
    u,
    r4,
    load_sem,
    in_send,
    in_recv,
    halo_send,
    halo_recv,
    own_sem,
    send1,
    recv1,
    send2,
    recv2,
    send3,
    recv3,
    send4,
    recv4,
):
    loads = [
        pltpu.make_async_copy(src, dst, load_sem.at[n])
        for n, (src, dst) in enumerate(
            (
                (x_ref, xin),
                (dy_ref, dyin),
                (gain_ref, gain_v),
                (ids_ref, ids_in),
                (wqkv_ref, wqkv),
                (wproj_ref, wproj),
            )
        )
    ]
    for n in (0, 1, 3):
        loads[n].start()

    lat, lon, dp = place()
    y_hi, z = lat // 8, lax.rem(lat, 8)
    y_lo, chip_core = lon // 2, lax.rem(lon, 2)
    y_pos = 2 * y_hi + y_lo
    pair = (lat, y_lo * 2 + 1 - chip_core, dp)
    along_x = [lax.rem(dp + k, 4) for k in range(1, 4)]
    x_devices = [(lat, lon, other) for other in along_x]
    along_y = []
    for k in range(1, 4):
        other = lax.rem(y_pos + k, 4)
        along_y.append((other // 2, lax.rem(other, 2)))
    y_devices = [(hi * 8 + z, lo * 2 + chip_core, dp) for hi, lo in along_y]
    along_z = [lax.rem(z + k, 8) for k in range(1, 8)]
    z_devices = [(y_hi * 8 + other, lon, dp) for other in along_z]
    odd, to, source, sent, taken, own = partners()
    barrier = pltpu.get_barrier_semaphore()
    for device in to + source + [pair] + x_devices + y_devices + z_devices:
        pl.semaphore_signal(barrier, inc=1, device_id=device, device_id_type=MESH)

    for n in (0, 1, 3):
        loads[n].wait()
    pl.semaphore_wait(barrier, 3 + 3 + 1 + 3 + 3 + 7)
    arriving = [[], []]
    local = []
    for n, (src, dst) in enumerate(((xin, xv), (dyin, dyv))):
        for k in range(3):
            sems = (in_send.at[3 * n + k], in_recv.at[3 * n + k])
            arriving[n].append(remote(block_part(src, sent[k]), window_part(dst, sent[k]), *sems, to[k]))
        local.append(pltpu.make_async_copy(block_part(src, own), window_part(dst, own), own_sem.at[n]))
        send_all(arriving[n] + local[n:])
    for n in (2, 4, 5):
        loads[n].start()

    @pl.when(odd == 1)
    def _():
        labels = remote(ids_in, ids, in_send.at[6], in_recv.at[6], to[0])
        labels.start()
        labels.wait()

    @pl.when(odd == 0)
    def _():
        labels = pltpu.make_async_copy(ids_in, ids, own_sem.at[2])
        labels.start()
        labels.wait()

    window_masks(ids, same)
    loads[2].wait()
    take_all(arriving[0])
    local[0].wait()
    gain = gain_v[...]
    spread(xv, wide)
    for level in range(LEV):
        x = load_level(wide, level)
        centred = x - jnp.mean(x, axis=-1, keepdims=True)
        inv_std = lax.rsqrt(jnp.mean(centred * centred, axis=-1, keepdims=True) + 1e-05)
        unit = centred * inv_std
        xs[rows_of(level), :] = x
        normed[rows_of(level), :] = unit
        inv[rows_of(level), :] = jnp.broadcast_to(inv_std, (CELLS, 128))
        hid[rows_of(level), :] = (unit * gain).astype(BF16)
    take_all(arriving[1])
    local[1].wait()
    spread(dyv, wide)
    for level in range(LEV):
        dys[rows_of(level), :] = load_level(wide, level).astype(BF16)
    loads[4].wait()
    qkv[...] = dot(hid[...], wqkv[...]).astype(BF16)
    loads[5].wait()
    datt[...] = dot_nt(dys[...], wproj[...]).astype(BF16)
    hid_t[...] = hid[...].T
    dys_t[...] = dys[...].T

    def attend(h):
        for w in range(2):
            head_pair(w, h, qkv, datt, same, att, dqkv)

    def grad_chunk(h):
        at = h * 128
        left = jnp.concatenate([dqkv[:, n * ATT + at : n * ATT + at + 128] for n in range(3)], axis=1)
        right = att[:, at : at + 128]

        for n in range(2):
            rows = pl.ds(512 * n, 512)
            part = jnp.concatenate((dot(hid_t[rows, :], left), dot(dys_t[rows, :], right)), axis=1)
            gbuf[h, 8 * n : 8 * n + 8] = part.astype(BF16).reshape(8, 2, 2, 16, WIDE)

    def send_pair(h):
        copy = remote(gbuf.at[h, :, :, 1 - chip_core], r1.at[h], send1.at[h], recv1.at[h], pair)
        copy.start()
        return [copy]

    def add_pair(h):
        s = SLOT[h]

        def step(n, _):
            i, j = n // 2, lax.rem(n, 2)
            total = gbuf[h, i, j, chip_core] + r1[h, i, j]
            if FIRST_AXIS[h] == 'x':
                for k in range(4):
                    sx[s, k, i // 8, lax.rem(i, 8), j] = total[4 * k : 4 * k + 4]
            else:
                sy[s, i // 8, lax.rem(i, 8), j] = total
            return 0

        lax.fori_loop(0, 32, step, 0, unroll=8)
        copies = []
        for k in range(3):
            sems = (send2.at[h, k], recv2.at[h, k])
            if FIRST_AXIS[h] == 'x':
                copies.append(remote(sx.at[s, along_x[k]], r2x.at[s, k], *sems, x_devices[k]))
            else:
                hi, lo = along_y[k]
                copies.append(remote(sy.at[s, hi, :, lo], r2y.at[s, k], *sems, y_devices[k]))
        return send_all(copies)

    def add_second(h):
        s = SLOT[h]
        if FIRST_AXIS[h] == 'x':

            def step(n, _):
                hi, i, j = n // 16, lax.rem(n // 2, 8), lax.rem(n, 2)
                total = sx[s, dp, hi, i, j].astype(F32)
                for k in range(3):
                    total = total + r2x[s, k, hi, i, j].astype(F32)
                tx[s, hi, i, j] = total.astype(BF16)
                return 0

            lax.fori_loop(0, 32, step, 0, unroll=8)
        else:

            def step(i, _):
                total = sy[s, y_hi, i, y_lo].astype(F32)
                for k in range(3):
                    total = total + r2y[s, k, i].astype(F32)
                for k in range(4):
                    ty[s, k, i] = total[4 * k : 4 * k + 4].astype(BF16)
                return 0

            lax.fori_loop(0, 8, step, 0, unroll=4)
        copies = []
        for k in range(3):
            sems = (send3.at[h, k], recv3.at[h, k])
            if FIRST_AXIS[h] == 'x':
                hi, lo = along_y[k]
                copies.append(remote(tx.at[s, hi, :, lo], r3.at[h, k], *sems, y_devices[k]))
            else:
                copies.append(remote(ty.at[s, along_x[k]], r3.at[h, k], *sems, x_devices[k]))
        return send_all(copies)

    def add_third(h):
        s = SLOT[h]

        def step(i, _):
            total = (tx[s, y_hi, i, y_lo] if FIRST_AXIS[h] == 'x' else ty[s, dp, i]).astype(F32)
            for k in range(3):
                total = total + r3[h, k, i].astype(F32)
            u[i, :, WIDE * h : WIDE * h + WIDE] = total.astype(BF16)
            return 0

        lax.fori_loop(0, 8, step, 0, unroll=4)

    def send_last():
        return send_all(
            [remote(u.at[along_z[k]], r4.at[k], send4.at[k], recv4.at[k], z_devices[k]) for k in range(7)]
        )

    def add_last():
        total = u[z].astype(F32)
        for k in range(7):
            total = total + r4[k].astype(F32)
        total = total * (1.0 / math.sqrt(73728))
        for h in range(CHUNKS):
            for n in range(3):
                at = WIDE * h + 128 * n
                qkv_out[:, n * ATT + 128 * h : n * ATT + 128 * h + 128] = total[:, at : at + 128]
            proj_out[:, 128 * h : 128 * h + 128] = total[:, WIDE * h + 384 : WIDE * h + 512]

    def send_back(n, src, dst):
        copies = [
            remote(
                window_part(src, taken[k]),
                block_part(dst, taken[k]),
                halo_send.at[3 * n + k],
                halo_recv.at[3 * n + k],
                source[k],
            )
            for k in range(3)
        ]
        copies.append(pltpu.make_async_copy(window_part(src, own), block_part(dst, own), own_sem.at[3 + n]))
        return send_all(copies)

    first, second, third = [None] * 4, [None] * 4, [None] * 4
    for h in range(CHUNKS):
        attend(h)
        if h > 0:
            take_all(first[h - 1])
            second[h - 1] = add_pair(h - 1)
        grad_chunk(h)
        first[h] = send_pair(h)

    xs[...] += dot(att[...], wproj[...])
    take_all(first[3])
    second[3] = add_pair(3)
    for level in range(LEV):
        store_level(wide, level, xs[rows_of(level), :])
    gather(wide, xv)
    back = send_back(0, xv, y_ref)
    xs[...] = dot_nt(dqkv[...], wqkv[...])
    for level in range(LEV):
        g = xs[rows_of(level), :] * gain
        unit = normed[rows_of(level), :]
        correction = g - jnp.mean(g, axis=-1, keepdims=True) - unit * jnp.mean(g * unit, axis=-1, keepdims=True)
        inv_std = inv[rows_of(level), 0:1]
        store_level(wide, level, dys[rows_of(level), :].astype(F32) + inv_std * correction)
    gather(wide, dyv)
    back += send_back(1, dyv, dx_ref)
    for h in range(CHUNKS):
        take_all(second[h])
        third[h] = add_second(h)
    for h in range(CHUNKS):
        take_all(third[h])
        add_third(h)
    fourth = send_last()
    group = lat * 4 + lon
    block = wqkv[pl.ds(pl.multiple_of(16 * group, 16), 16), :].astype(F32)
    w_rows = jnp.zeros((4, QKV), F32)
    for k in range(4):
        w_rows = w_rows + jnp.where(dp == k, block[4 * k : 4 * k + 4], 0.0)
    lanes = lax.broadcasted_iota(jnp.int32, (4, 128), 1)
    rows = lax.broadcasted_iota(jnp.int32, (4, 128), 0)
    near = gain_v[:, pl.ds(pl.multiple_of(128 * (group // 8), 128), 128)]
    at = lax.rem(group, 8) * 16 + dp * 4
    gains = jnp.sum(jnp.where(lanes == at + rows, jnp.broadcast_to(near, (4, 128)), 0.0), axis=-1, keepdims=True)
    w_rows = w_rows / gains
    take_all(fourth)
    add_last()

    summed = jnp.broadcast_to(jnp.sum(w_rows * qkv_out[...], axis=-1, keepdims=True), (4, 128))
    gain_out[...] = jnp.sum(jnp.where(lanes == rows, summed, 0.0), axis=0, keepdims=True)
    for copies in arriving + first + second + third + [fourth]:
        for copy in copies:
            copy.wait_send()
    wait_all(back)


def send_all(copies):
    for copy in copies:
        copy.start()
    return copies


def take_all(copies):
    for copy in copies:
        copy.wait_recv()


def wait_all(copies):
    for copy in copies:
        copy.wait()


def core(x, dy, ids, gain, w_qkv, w_proj):
    block = jax.ShapeDtypeStruct((WA, WO, LEV, D), BF16)
    any_space = pl.BlockSpec(memory_space=pl.ANY)
    vmem = pl.BlockSpec(memory_space=pltpu.VMEM)
    dma = pltpu.SemaphoreType.DMA
    return pl.pallas_call(
        core_kernel,
        out_shape=(
            block,
            block,
            jax.ShapeDtypeStruct((4, QKV), F32),
            jax.ShapeDtypeStruct((4, ATT), F32),
            jax.ShapeDtypeStruct((1, 128), F32),
        ),
        in_specs=[any_space] * 6,
        out_specs=(any_space, any_space, vmem, vmem, vmem),
        scratch_shapes=[
            pltpu.VMEM((WA, WO, LEV, D), BF16),
            pltpu.VMEM((WA, WO, LEV, D), BF16),
            pltpu.VMEM((WA, WO, LEV, D), BF16),
            pltpu.VMEM((WA, WO, LEV, D), BF16),
            pltpu.VMEM((WO, LEV, WA), jnp.int32),
            pltpu.VMEM((WO, LEV, WA), jnp.int32),
            pltpu.VMEM((1, D), F32),
            pltpu.VMEM((D, QKV), BF16),
            pltpu.VMEM((ATT, D), BF16),
            pltpu.VMEM((D // 128, ROWS, 128), F32),
            pltpu.VMEM((ROWS, D), F32),
            pltpu.VMEM((ROWS, D), F32),
            pltpu.VMEM((ROWS, 128), F32),
            pltpu.VMEM((ROWS, D), BF16),
            pltpu.VMEM((ROWS, D), BF16),
            pltpu.VMEM((D, ROWS), BF16),
            pltpu.VMEM((D, ROWS), BF16),
            pltpu.VMEM((ROWS, QKV), BF16),
            pltpu.VMEM((ROWS, ATT), BF16),
            pltpu.VMEM((ROWS, ATT), BF16),
            pltpu.VMEM((ROWS, QKV), BF16),
            pltpu.VMEM((2, SPAN, 2 * SPAN), F32),
            pltpu.VMEM((4, 16, 2, 2, 16, WIDE), BF16),
            pltpu.VMEM((4, 16, 2, 16, WIDE), BF16),
            pltpu.VMEM((3, 4, 2, 8, 2, 4, WIDE), BF16),
            pltpu.VMEM((2, 2, 8, 2, 16, WIDE), BF16),
            pltpu.VMEM((3, 3, 2, 8, 2, 4, WIDE), BF16),
            pltpu.VMEM((2, 3, 8, 16, WIDE), BF16),
            pltpu.VMEM((3, 2, 8, 2, 4, WIDE), BF16),
            pltpu.VMEM((2, 4, 8, 4, WIDE), BF16),
            pltpu.VMEM((4, 3, 8, 4, WIDE), BF16),
            pltpu.VMEM((8, 4, COLS), BF16),
            pltpu.VMEM((7, 4, COLS), BF16),
            dma((6,)),
            dma((7,)),
            dma((7,)),
            dma((6,)),
            dma((6,)),
            dma((5,)),
            dma((4,)),
            dma((4,)),
            dma((4, 3)),
            dma((4, 3)),
            dma((4, 3)),
            dma((4, 3)),
            dma((7,)),
            dma((7,)),
        ],
        compiler_params=pltpu.CompilerParams(
            collective_id=1, has_side_effects=True, vmem_limit_bytes=56 * 2**20
        ),
        name="window_attention",
    )(x, dy, ids, gain, w_qkv, w_proj)


def finish_kernel(*refs):
    arrays, results, held, (sems,) = refs[:5], refs[5:10], refs[10:15], refs[15:]
    taken = send_all([pltpu.make_async_copy(arrays[n], held[n], sems.at[n]) for n in range(5)])
    put = []
    for n in range(4):
        taken[n].wait()
        put += send_all([pltpu.make_async_copy(held[n], results[n], sems.at[5 + n])])
    taken[4].wait()
    results[4][...] = held[4][:, :4]
    wait_all(put)


def finish(*arrays):
    any_space = pl.BlockSpec(memory_space=pl.ANY)
    shapes = [jax.ShapeDtypeStruct(a.shape, a.dtype) for a in arrays[:4]] + [jax.ShapeDtypeStruct((1, 4), F32)]
    return pl.pallas_call(
        finish_kernel,
        out_shape=tuple(shapes),
        in_specs=[any_space] * 5,
        out_specs=(any_space,) * 4 + (pl.BlockSpec(memory_space=pltpu.VMEM),),
        scratch_shapes=[pltpu.VMEM(a.shape, a.dtype) for a in arrays] + [pltpu.SemaphoreType.DMA((9,))],
        compiler_params=pltpu.CompilerParams(vmem_limit_bytes=56 * 2**20),
        name="results",
    )(*arrays)


def cells_first(block):
    return block.transpose(0, 2, 3, 1, 4).reshape(WA, WO, LEV, D)


def on_device(inputs, cotangent, gain, w_qkv, w_proj, window_ids):
    y, dx, qkv_part, proj_part, gain_part = core(
        cells_first(inputs),
        cells_first(cotangent),
        window_ids.transpose(2, 0, 1),
        gain.reshape(1, D),
        w_qkv,
        w_proj,
    )
    y, dx, qkv_part, proj_part, gain_part = finish(y, dx, qkv_part, proj_part, gain_part)
    back = lambda block: block[None].transpose(0, 3, 1, 2, 4)
    return back(y), back(dx), qkv_part, proj_part.T, gain_part.reshape(4)


def solution(mesh):
    return jax.shard_map(
        on_device,
        mesh=mesh,
        in_specs=(
            P("dp", None, "lat", "lon", None),
            P("dp", None, "lat", "lon", None),
            P(),
            P(),
            P(),
            P(None, "lat", "lon"),
        ),
        out_specs=(
            P("dp", None, "lat", "lon", None),
            P("dp", None, "lat", "lon", None),
            P(("lat", "lon", "dp"), None),
            P(None, ("lat", "lon", "dp")),
            P(("lat", "lon", "dp")),
        ),
        check_vma=False,
    )
```

```python
import functools
import math

import jax
import jax.numpy as jnp
from jax import lax
from jax.experimental import pallas as pl
from jax.experimental.pallas import tpu as pltpu
from jax.sharding import PartitionSpec as P

HEADS = 8
HSZ = 64
WA = 12
WO = 6
HALF_A = WA // 2
HALF_O = WO // 2
LEV = 4
CELLS = WA * WO
ROWS = CELLS * LEV
SPAN = 2 * CELLS
D = 1024
QKV = 3 * HEADS * HSZ
ATT = HEADS * HSZ
COLS = QKV + ATT
CHUNKS = HEADS // 2
WIDE = COLS // CHUNKS
FIRST_AXIS = 'xyxx'
SLOT = [FIRST_AXIS[:h].count(FIRST_AXIS[h]) for h in range(CHUNKS)]
MESH = pl.DeviceIdType.MESH
F32 = jnp.float32
BF16 = jnp.bfloat16


def place():
    return lax.axis_index("lat"), lax.axis_index("lon"), lax.axis_index("dp")


def wrap(value, size):
    return lax.rem(value + size, size)


def later(lon):
    return 1 - lax.rem(lon, 2)


def partners():
    lat, lon, dp = place()
    west, east = wrap(lon - 1, 4), wrap(lon + 1, 4)
    here, there = later(lon), later(west)
    to = [(wrap(lat + 2 * here - 1, 16), lon, dp), (lat, west, dp), (wrap(lat + 2 * there - 1, 16), west, dp)]
    other = wrap(lat + 1 - 2 * here, 16)
    source = [(other, lon, dp), (lat, east, dp), (other, east, dp)]
    sent = [(here, 1), (1 - there, 0), (there, 0)]
    taken = [(here, 1), (1 - here, 0), (here, 0)]
    own = (1 - here, 1)
    return here, to, source, sent, taken, own


def block_part(ref, part):
    return ref.at[pl.ds(part[0] * HALF_A, HALF_A), pl.ds(part[1] * HALF_O, HALF_O)]


def window_part(ref, part):
    return ref.at[pl.ds((1 - part[0]) * HALF_A, HALF_A), pl.ds((1 - part[1]) * HALF_O, HALF_O)]


def remote(src, dst, send_sem, recv_sem, device):
    return pltpu.make_async_remote_copy(
        src_ref=src, dst_ref=dst, send_sem=send_sem, recv_sem=recv_sem, device_id=device, device_id_type=MESH
    )


def dot(a, b):
    return jnp.dot(a, b, preferred_element_type=F32)


def dot_nt(a, b):
    return lax.dot_general(a, b, (((1,), (1,)), ((), ())), preferred_element_type=F32)


def dot_tn(a, b):
    return lax.dot_general(a, b, (((0,), (0,)), ((), ())), preferred_element_type=F32)


def spread(block_ref, wide):
    def step(r, _):
        for c in range(WO // 2):
            pair = jnp.concatenate((block_ref[r, 2 * c].astype(F32), block_ref[r, 2 * c + 1].astype(F32)), axis=0)
            at = pl.multiple_of(24 * r + 8 * c, 8)
            for j in range(D // 128):
                wide[j, pl.ds(at, 8), :] = pair[:, 128 * j : 128 * j + 128]
        return 0

    lax.fori_loop(0, WA, step, 0, unroll=2)


def gather(wide, block_ref):
    def step(r, _):
        for c in range(WO // 2):
            at = pl.multiple_of(24 * r + 8 * c, 8)
            pair = jnp.concatenate([wide[j, pl.ds(at, 8), :] for j in range(D // 128)], axis=1)
            block_ref[r, 2 * c] = pair[:LEV].astype(BF16)
            block_ref[r, 2 * c + 1] = pair[LEV:].astype(BF16)
        return 0

    lax.fori_loop(0, WA, step, 0, unroll=2)


def load_level(wide, level):
    return jnp.concatenate([wide[j, pl.ds(level, CELLS, stride=LEV), :] for j in range(D // 128)], axis=1)


def store_level(wide, level, value):
    for j in range(D // 128):
        wide[j, pl.ds(level, CELLS, stride=LEV), :] = value[:, 128 * j : 128 * j + 128]


def rows_of(level):
    return pl.ds(level * CELLS, CELLS)


def window_masks(ids, same):
    labels = jnp.zeros((LEV, 128), F32)
    for c in range(WO):
        row = lax.broadcasted_iota(jnp.int32, (WA, 128), 0)
        cell = lax.broadcasted_iota(jnp.int32, (WA, 128), 1)
        place_of = jnp.where(cell == WO * row + c, 1.0, 0.0)
        labels = labels + dot(ids[c].astype(F32), place_of)
    for w in range(2):
        row = jnp.broadcast_to(labels[2 * w : 2 * w + 1, :], (128, 128))
        one = (row == row.T)[:CELLS, :CELLS].astype(F32)
        four = jnp.concatenate((one, one, one, one), axis=1)
        same[w] = jnp.concatenate((four, four), axis=0)


def head_pair(w, h, qkv, datt, same, att, dqkv):
    low = lax.broadcasted_iota(jnp.int32, (1, 128), 1) < HSZ
    rows = pl.ds(w * SPAN, SPAN)
    at = h * 128
    q2 = qkv[rows, pl.ds(at, 128)]
    k2 = qkv[rows, pl.ds(ATT + at, 128)]
    v2 = qkv[rows, pl.ds(2 * ATT + at, 128)]
    o2 = datt[rows, pl.ds(at, 128)]
    low_w = jnp.broadcast_to(low, (SPAN, 128))

    def split(x, scale=1.0):
        x = x.astype(F32) * scale
        return jnp.concatenate((jnp.where(low_w, x, 0.0), jnp.where(low_w, 0.0, x)), axis=0).astype(BF16)

    q4 = split(q2)
    o4 = split(o2)
    scores = jnp.where(same[w] > 0.5, dot_nt(k2, split(q2, HSZ**-0.5)), -1e30)
    scores = scores - jnp.max(scores, axis=0, keepdims=True)
    weight = jnp.exp(scores)
    prob = weight * (1.0 / jnp.sum(weight, axis=0, keepdims=True))
    prob_b = prob.astype(BF16)
    d_prob = dot_nt(v2, o4)
    inner = jnp.sum(prob * d_prob, axis=0, keepdims=True)
    d_score = (prob * (d_prob - inner) * (HSZ**-0.5)).astype(BF16)
    two_att = dot_tn(prob_b, v2)
    two_dq = dot_tn(d_score, k2)
    both = [
        jnp.where(low, two_att[:SPAN], two_att[SPAN:]).astype(BF16),
        jnp.where(low, two_dq[:SPAN], two_dq[SPAN:]).astype(BF16),
        dot(d_score, q4).astype(BF16),
        dot(prob_b, o4).astype(BF16),
    ]
    att[rows, pl.ds(at, 128)] = both[0]
    dqkv[rows, pl.ds(at, 128)] = both[1]
    dqkv[rows, pl.ds(ATT + at, 128)] = both[2]
    dqkv[rows, pl.ds(2 * ATT + at, 128)] = both[3]


def core_kernel(
    x_ref,
    dy_ref,
    ids_ref,
    gain_ref,
    wqkv_ref,
    wproj_ref,
    y_ref,
    dx_ref,
    qkv_out,
    proj_out,
    gain_out,
    xin,
    dyin,
    xv,
    dyv,
    ids,
    ids_in,
    gain_v,
    wqkv,
    wproj,
    wide,
    xs,
    normed,
    inv,
    hid,
    dys,
    hid_t,
    dys_t,
    qkv,
    datt,
    att,
    dqkv,
    same,
    gbuf,
    r1,
    sx,
    sy,
    r2x,
    r2y,
    tx,
    ty,
    r3,
    u,
    r4,
    load_sem,
    in_send,
    in_recv,
    halo_send,
    halo_recv,
    own_sem,
    send1,
    recv1,
    send2,
    recv2,
    send3,
    recv3,
    send4,
    recv4,
):
    loads = [
        pltpu.make_async_copy(src, dst, load_sem.at[n])
        for n, (src, dst) in enumerate(
            (
                (x_ref, xin),
                (dy_ref, dyin),
                (gain_ref, gain_v),
                (ids_ref, ids_in),
                (wqkv_ref, wqkv),
                (wproj_ref, wproj),
            )
        )
    ]
    for copy in loads:
        copy.start()

    lat, lon, dp = place()
    y_hi, z = lat // 8, lax.rem(lat, 8)
    y_lo, chip_core = lon // 2, lax.rem(lon, 2)
    y_pos = 2 * y_hi + y_lo
    pair = (lat, y_lo * 2 + 1 - chip_core, dp)
    along_x = [lax.rem(dp + k, 4) for k in range(1, 4)]
    x_devices = [(lat, lon, other) for other in along_x]
    along_y = []
    for k in range(1, 4):
        other = lax.rem(y_pos + k, 4)
        along_y.append((other // 2, lax.rem(other, 2)))
    y_devices = [(hi * 8 + z, lo * 2 + chip_core, dp) for hi, lo in along_y]
    along_z = [lax.rem(z + k, 8) for k in range(1, 8)]
    z_devices = [(y_hi * 8 + other, lon, dp) for other in along_z]
    odd, to, source, sent, taken, own = partners()
    barrier = pltpu.get_barrier_semaphore()
    for device in to + source + [pair] + x_devices + y_devices + z_devices:
        pl.semaphore_signal(barrier, inc=1, device_id=device, device_id_type=MESH)

    for n in (0, 1, 3):
        loads[n].wait()
    pl.semaphore_wait(barrier, 3 + 3 + 1 + 3 + 3 + 7)
    arriving = [[], []]
    local = []
    for n, (src, dst) in enumerate(((xin, xv), (dyin, dyv))):
        for k in range(3):
            sems = (in_send.at[3 * n + k], in_recv.at[3 * n + k])
            arriving[n].append(remote(block_part(src, sent[k]), window_part(dst, sent[k]), *sems, to[k]))
        local.append(pltpu.make_async_copy(block_part(src, own), window_part(dst, own), own_sem.at[n]))
        send_all(arriving[n] + local[n:])

    @pl.when(odd == 1)
    def _():
        labels = remote(ids_in, ids, in_send.at[6], in_recv.at[6], to[0])
        labels.start()
        labels.wait()

    @pl.when(odd == 0)
    def _():
        labels = pltpu.make_async_copy(ids_in, ids, own_sem.at[2])
        labels.start()
        labels.wait()

    window_masks(ids, same)
    loads[2].wait()
    take_all(arriving[0])
    local[0].wait()
    gain = gain_v[...]
    spread(xv, wide)
    for level in range(LEV):
        x = load_level(wide, level)
        centred = x - jnp.mean(x, axis=-1, keepdims=True)
        inv_std = lax.rsqrt(jnp.mean(centred * centred, axis=-1, keepdims=True) + 1e-05)
        unit = centred * inv_std
        xs[rows_of(level), :] = x
        normed[rows_of(level), :] = unit
        inv[rows_of(level), :] = jnp.broadcast_to(inv_std, (CELLS, 128))
        hid[rows_of(level), :] = (unit * gain).astype(BF16)
    loads[4].wait()
    qkv[...] = dot(hid[...], wqkv[...]).astype(BF16)
    hid_t[...] = hid[...].T
    take_all(arriving[1])
    local[1].wait()
    spread(dyv, wide)
    for level in range(LEV):
        dys[rows_of(level), :] = load_level(wide, level).astype(BF16)
    loads[5].wait()
    datt[...] = dot_nt(dys[...], wproj[...]).astype(BF16)
    dys_t[...] = dys[...].T

    def attend(h):
        for w in range(2):
            head_pair(w, h, qkv, datt, same, att, dqkv)

    def grad_chunk(h):
        at = h * 128
        left = jnp.concatenate([dqkv[:, n * ATT + at : n * ATT + at + 128] for n in range(3)], axis=1)
        right = att[:, at : at + 128]

        for n in range(2):
            rows = pl.ds(512 * n, 512)
            part = jnp.concatenate((dot(hid_t[rows, :], left), dot(dys_t[rows, :], right)), axis=1)
            gbuf[h, 8 * n : 8 * n + 8] = part.astype(BF16).reshape(8, 2, 2, 16, WIDE)

    def send_pair(h):
        copy = remote(gbuf.at[h, :, :, 1 - chip_core], r1.at[h], send1.at[h], recv1.at[h], pair)
        copy.start()
        return [copy]

    def add_pair(h):
        s = SLOT[h]

        def step(n, _):
            i, j = n // 2, lax.rem(n, 2)
            total = gbuf[h, i, j, chip_core] + r1[h, i, j]
            if FIRST_AXIS[h] == 'x':
                for k in range(4):
                    sx[s, k, i // 8, lax.rem(i, 8), j] = total[4 * k : 4 * k + 4]
            else:
                sy[s, i // 8, lax.rem(i, 8), j] = total
            return 0

        lax.fori_loop(0, 32, step, 0, unroll=8)
        copies = []
        for k in range(3):
            sems = (send2.at[h, k], recv2.at[h, k])
            if FIRST_AXIS[h] == 'x':
                copies.append(remote(sx.at[s, along_x[k]], r2x.at[s, k], *sems, x_devices[k]))
            else:
                hi, lo = along_y[k]
                copies.append(remote(sy.at[s, hi, :, lo], r2y.at[s, k], *sems, y_devices[k]))
        return send_all(copies)

    def add_second(h):
        s = SLOT[h]
        if FIRST_AXIS[h] == 'x':

            def step(n, _):
                hi, i, j = n // 16, lax.rem(n // 2, 8), lax.rem(n, 2)
                total = sx[s, dp, hi, i, j].astype(F32)
                for k in range(3):
                    total = total + r2x[s, k, hi, i, j].astype(F32)
                tx[s, hi, i, j] = total.astype(BF16)
                return 0

            lax.fori_loop(0, 32, step, 0, unroll=8)
        else:

            def step(i, _):
                total = sy[s, y_hi, i, y_lo].astype(F32)
                for k in range(3):
                    total = total + r2y[s, k, i].astype(F32)
                for k in range(4):
                    ty[s, k, i] = total[4 * k : 4 * k + 4].astype(BF16)
                return 0

            lax.fori_loop(0, 8, step, 0, unroll=4)
        copies = []
        for k in range(3):
            sems = (send3.at[h, k], recv3.at[h, k])
            if FIRST_AXIS[h] == 'x':
                hi, lo = along_y[k]
                copies.append(remote(tx.at[s, hi, :, lo], r3.at[h, k], *sems, y_devices[k]))
            else:
                copies.append(remote(ty.at[s, along_x[k]], r3.at[h, k], *sems, x_devices[k]))
        return send_all(copies)

    def add_third(h):
        s = SLOT[h]

        def step(i, _):
            total = (tx[s, y_hi, i, y_lo] if FIRST_AXIS[h] == 'x' else ty[s, dp, i]).astype(F32)
            for k in range(3):
                total = total + r3[h, k, i].astype(F32)
            u[i, :, WIDE * h : WIDE * h + WIDE] = total.astype(BF16)
            return 0

        lax.fori_loop(0, 8, step, 0, unroll=4)

    def send_last():
        return send_all(
            [remote(u.at[along_z[k]], r4.at[k], send4.at[k], recv4.at[k], z_devices[k]) for k in range(7)]
        )

    def add_last():
        total = u[z].astype(F32)
        for k in range(7):
            total = total + r4[k].astype(F32)
        total = total * (1.0 / math.sqrt(73728))
        for h in range(CHUNKS):
            for n in range(3):
                at = WIDE * h + 128 * n
                qkv_out[:, n * ATT + 128 * h : n * ATT + 128 * h + 128] = total[:, at : at + 128]
            proj_out[:, 128 * h : 128 * h + 128] = total[:, WIDE * h + 384 : WIDE * h + 512]

    def send_back(n, src, dst):
        copies = [
            remote(
                window_part(src, taken[k]),
                block_part(dst, taken[k]),
                halo_send.at[3 * n + k],
                halo_recv.at[3 * n + k],
                source[k],
            )
            for k in range(3)
        ]
        copies.append(pltpu.make_async_copy(window_part(src, own), block_part(dst, own), own_sem.at[3 + n]))
        return send_all(copies)

    first, second, third = [None] * 4, [None] * 4, [None] * 4
    for h in range(CHUNKS):
        attend(h)
        if h > 0:
            take_all(first[h - 1])
            second[h - 1] = add_pair(h - 1)
        grad_chunk(h)
        first[h] = send_pair(h)

    xs[...] += dot(att[...], wproj[...])
    take_all(first[3])
    second[3] = add_pair(3)
    for level in range(LEV):
        store_level(wide, level, xs[rows_of(level), :])
    gather(wide, xv)
    back = send_back(0, xv, y_ref)
    xs[...] = dot_nt(dqkv[...], wqkv[...])
    for level in range(LEV):
        g = xs[rows_of(level), :] * gain
        unit = normed[rows_of(level), :]
        correction = g - jnp.mean(g, axis=-1, keepdims=True) - unit * jnp.mean(g * unit, axis=-1, keepdims=True)
        inv_std = inv[rows_of(level), 0:1]
        store_level(wide, level, dys[rows_of(level), :].astype(F32) + inv_std * correction)
    gather(wide, dyv)
    back += send_back(1, dyv, dx_ref)
    for h in range(CHUNKS):
        take_all(second[h])
        third[h] = add_second(h)
    for h in range(CHUNKS):
        take_all(third[h])
        add_third(h)
    fourth = send_last()
    group = lat * 4 + lon
    block = wqkv[pl.ds(pl.multiple_of(16 * group, 16), 16), :].astype(F32)
    w_rows = jnp.zeros((4, QKV), F32)
    for k in range(4):
        w_rows = w_rows + jnp.where(dp == k, block[4 * k : 4 * k + 4], 0.0)
    lanes = lax.broadcasted_iota(jnp.int32, (4, 128), 1)
    rows = lax.broadcasted_iota(jnp.int32, (4, 128), 0)
    near = gain_v[:, pl.ds(pl.multiple_of(128 * (group // 8), 128), 128)]
    at = lax.rem(group, 8) * 16 + dp * 4
    gains = jnp.sum(jnp.where(lanes == at + rows, jnp.broadcast_to(near, (4, 128)), 0.0), axis=-1, keepdims=True)
    w_rows = w_rows / gains
    take_all(fourth)
    add_last()

    summed = jnp.broadcast_to(jnp.sum(w_rows * qkv_out[...], axis=-1, keepdims=True), (4, 128))
    gain_out[...] = jnp.sum(jnp.where(lanes == rows, summed, 0.0), axis=0, keepdims=True)
    for copies in arriving + first + second + third + [fourth]:
        for copy in copies:
            copy.wait_send()
    wait_all(back)


def send_all(copies):
    for copy in copies:
        copy.start()
    return copies


def take_all(copies):
    for copy in copies:
        copy.wait_recv()


def wait_all(copies):
    for copy in copies:
        copy.wait()


def core(x, dy, ids, gain, w_qkv, w_proj):
    block = jax.ShapeDtypeStruct((WA, WO, LEV, D), BF16)
    any_space = pl.BlockSpec(memory_space=pl.ANY)
    vmem = pl.BlockSpec(memory_space=pltpu.VMEM)
    dma = pltpu.SemaphoreType.DMA
    return pl.pallas_call(
        core_kernel,
        out_shape=(
            block,
            block,
            jax.ShapeDtypeStruct((4, QKV), F32),
            jax.ShapeDtypeStruct((4, ATT), F32),
            jax.ShapeDtypeStruct((1, 128), F32),
        ),
        in_specs=[any_space] * 6,
        out_specs=(any_space, any_space, vmem, vmem, vmem),
        scratch_shapes=[
            pltpu.VMEM((WA, WO, LEV, D), BF16),
            pltpu.VMEM((WA, WO, LEV, D), BF16),
            pltpu.VMEM((WA, WO, LEV, D), BF16),
            pltpu.VMEM((WA, WO, LEV, D), BF16),
            pltpu.VMEM((WO, LEV, WA), jnp.int32),
            pltpu.VMEM((WO, LEV, WA), jnp.int32),
            pltpu.VMEM((1, D), F32),
            pltpu.VMEM((D, QKV), BF16),
            pltpu.VMEM((ATT, D), BF16),
            pltpu.VMEM((D // 128, ROWS, 128), F32),
            pltpu.VMEM((ROWS, D), F32),
            pltpu.VMEM((ROWS, D), F32),
            pltpu.VMEM((ROWS, 128), F32),
            pltpu.VMEM((ROWS, D), BF16),
            pltpu.VMEM((ROWS, D), BF16),
            pltpu.VMEM((D, ROWS), BF16),
            pltpu.VMEM((D, ROWS), BF16),
            pltpu.VMEM((ROWS, QKV), BF16),
            pltpu.VMEM((ROWS, ATT), BF16),
            pltpu.VMEM((ROWS, ATT), BF16),
            pltpu.VMEM((ROWS, QKV), BF16),
            pltpu.VMEM((2, SPAN, 2 * SPAN), F32),
            pltpu.VMEM((4, 16, 2, 2, 16, WIDE), BF16),
            pltpu.VMEM((4, 16, 2, 16, WIDE), BF16),
            pltpu.VMEM((3, 4, 2, 8, 2, 4, WIDE), BF16),
            pltpu.VMEM((2, 2, 8, 2, 16, WIDE), BF16),
            pltpu.VMEM((3, 3, 2, 8, 2, 4, WIDE), BF16),
            pltpu.VMEM((2, 3, 8, 16, WIDE), BF16),
            pltpu.VMEM((3, 2, 8, 2, 4, WIDE), BF16),
            pltpu.VMEM((2, 4, 8, 4, WIDE), BF16),
            pltpu.VMEM((4, 3, 8, 4, WIDE), BF16),
            pltpu.VMEM((8, 4, COLS), BF16),
            pltpu.VMEM((7, 4, COLS), BF16),
            dma((6,)),
            dma((7,)),
            dma((7,)),
            dma((6,)),
            dma((6,)),
            dma((5,)),
            dma((4,)),
            dma((4,)),
            dma((4, 3)),
            dma((4, 3)),
            dma((4, 3)),
            dma((4, 3)),
            dma((7,)),
            dma((7,)),
        ],
        compiler_params=pltpu.CompilerParams(
            collective_id=1, has_side_effects=True, vmem_limit_bytes=56 * 2**20
        ),
        name="window_attention",
    )(x, dy, ids, gain, w_qkv, w_proj)


def finish_kernel(*refs):
    arrays, results, held, (sems,) = refs[:5], refs[5:10], refs[10:15], refs[15:]
    taken = send_all([pltpu.make_async_copy(arrays[n], held[n], sems.at[n]) for n in range(5)])
    put = []
    for n in range(4):
        taken[n].wait()
        put += send_all([pltpu.make_async_copy(held[n], results[n], sems.at[5 + n])])
    taken[4].wait()
    results[4][...] = held[4][:, :4]
    wait_all(put)


def finish(*arrays):
    any_space = pl.BlockSpec(memory_space=pl.ANY)
    shapes = [jax.ShapeDtypeStruct(a.shape, a.dtype) for a in arrays[:4]] + [jax.ShapeDtypeStruct((1, 4), F32)]
    return pl.pallas_call(
        finish_kernel,
        out_shape=tuple(shapes),
        in_specs=[any_space] * 5,
        out_specs=(any_space,) * 4 + (pl.BlockSpec(memory_space=pltpu.VMEM),),
        scratch_shapes=[pltpu.VMEM(a.shape, a.dtype) for a in arrays] + [pltpu.SemaphoreType.DMA((9,))],
        compiler_params=pltpu.CompilerParams(vmem_limit_bytes=56 * 2**20),
        name="results",
    )(*arrays)


def cells_first(block):
    return block.transpose(0, 2, 3, 1, 4).reshape(WA, WO, LEV, D)


def on_device(inputs, cotangent, gain, w_qkv, w_proj, window_ids):
    y, dx, qkv_part, proj_part, gain_part = core(
        cells_first(inputs),
        cells_first(cotangent),
        window_ids.transpose(2, 0, 1),
        gain.reshape(1, D),
        w_qkv,
        w_proj,
    )
    y, dx, qkv_part, proj_part, gain_part = finish(y, dx, qkv_part, proj_part, gain_part)
    back = lambda block: block[None].transpose(0, 3, 1, 2, 4)
    return back(y), back(dx), qkv_part, proj_part.T, gain_part.reshape(4)


def solution(mesh):
    return jax.shard_map(
        on_device,
        mesh=mesh,
        in_specs=(
            P("dp", None, "lat", "lon", None),
            P("dp", None, "lat", "lon", None),
            P(),
            P(),
            P(),
            P(None, "lat", "lon"),
        ),
        out_specs=(
            P("dp", None, "lat", "lon", None),
            P("dp", None, "lat", "lon", None),
            P(("lat", "lon", "dp"), None),
            P(None, ("lat", "lon", "dp")),
            P(("lat", "lon", "dp")),
        ),
        check_vma=False,
    )
```
